32 devices in a mesh: gx: 8 (over y, x, core), gz: 4 (over z).
Axes of the slice: x: 2, y: 2, z: 4, core: 2. Of those that a mesh axis runs over, the one named last changes fastest.
Arguments:
- velocity: bfloat16 [2, 128, 2, 192, 512], P(None, None, None, 'gx', 'gz'), may hold values from -8 to 8
- snapshot_rank: int32 [128], replicated, may hold values from 0 to 127, each once
- anchor_index: int32 [64], replicated, may hold values from 0 to 196607
- start_basis: float32 [128, 64], replicated, may hold values from -6 to 6
Outputs:
- modes: bfloat16 [64, 2, 192, 512], P(None, None, 'gx', 'gz')
- basis: float32 [128, 64], replicated
The draws below stay inside these ranges and needn't reach their ends.
All inputs are finite; a program needn't handle non-finite values.
Results may differ from the reference program's by a relative error of at most 0.0073.
Values may be sent and summed in bfloat16 or wider, within the bound.
A program may use at most 64 MiB of HBM per device.

```python
import math
import jax
import jax.numpy as jnp
from jax import lax

M = 128
K = 64
P_SIZE = 2
ITERS = 3
NX = 192
NZ = 512
NCELLS = 196608


def draw_velocity(key, part):
    field_count = 32
    mixing_key = jax.random.fold_in(key, 101)
    stream_key = jax.random.fold_in(key, 202)
    span_key = jax.random.fold_in(key, 303)
    spread_key = jax.random.fold_in(key, 404)
    noise_key = jax.random.fold_in(key, 505)
    fields_key = jax.random.fold_in(key, 707)
    mixing = jax.random.normal(mixing_key, (M, field_count), jnp.float32) * (0.5 / math.sqrt(field_count))
    env_low = 0.5
    env_high = 2.0
    stream_envelope = jnp.exp(jax.random.uniform(stream_key, (field_count, NX), jnp.float32, math.log(env_low), math.log(env_high)))
    span_envelope = jnp.exp(jax.random.uniform(span_key, (field_count, NZ), jnp.float32, math.log(env_low), math.log(env_high)))
    spread = jnp.exp(jax.random.uniform(spread_key, (M,), jnp.float32, 0.0, math.log(1.6)))
    noise = jax.random.truncated_normal(noise_key, -6.0, 6.0, (2, M, P_SIZE, NX, NZ), jnp.float32)
    accumulated = noise * spread[None, :, None, None, None]

    def add_field(index, carried):
        field_key = jax.random.fold_in(fields_key, index)
        field = jax.random.truncated_normal(field_key, -6.0, 6.0, (2, P_SIZE, NX, NZ), jnp.float32)
        field = field * stream_envelope[index][None, None, :, None] * span_envelope[index][None, None, None, :]
        return carried + mixing[:, index][None, :, None, None, None] * field[:, None]
    accumulated = lax.fori_loop(0, field_count, add_field, accumulated)
    return jnp.clip(accumulated, -8.0, 8.0).astype(jnp.bfloat16)


def with_ends(drawn, rng, least, largest):
    index_at = [jax.random.randint(jax.random.fold_in(rng, axis), (), 0, length) for axis, length in enumerate(drawn.shape)]
    longest = drawn.shape.index(max(drawn.shape))
    next_to = index_at[:longest] + [(index_at[longest] + 1) % drawn.shape[longest]] + index_at[longest + 1:]
    return drawn.at[tuple(index_at)].set(least).at[tuple(next_to)].set(largest)


def centred(own_key, shape, width, limit, held_as=jnp.bfloat16):
    values = width * jax.random.normal(own_key, shape, jnp.float32)
    return jnp.clip(values, min=-limit, max=limit).astype(held_as)


def setup_inputs(seed: int = 0) -> dict:
    streams_of = jax.random.split(jax.random.key(seed), 5)
    return {
        "velocity": draw_velocity(jax.random.fold_in(streams_of[4], 71), 0),
        "snapshot_rank": jax.random.permutation(streams_of[1], M).astype(jnp.int32),
        "anchor_index": with_ends(jax.random.randint(streams_of[2], (K,), 0, NCELLS), jax.random.fold_in(streams_of[2], 1), 0, NCELLS - 1).astype(jnp.int32),
        "start_basis": centred(streams_of[3], (M, K), 1.0, 6.0, jnp.float32),
    }


def vorticity(field):
    upart = field[0].astype(jnp.float32)
    wpart = field[1].astype(jnp.float32)
    weights = (45.0 / 60.0, -9.0 / 60.0, 1.0 / 60.0)
    total = jnp.zeros(upart.shape, jnp.float32)
    for shift_by in range(1, 4):
        weight_now = weights[shift_by - 1]
        total = total + weight_now * (jnp.roll(wpart, -shift_by, axis=1) - jnp.roll(wpart, shift_by, axis=1))
        total = total - weight_now * (jnp.roll(upart, -shift_by, axis=2) - jnp.roll(upart, shift_by, axis=2))
    return total.astype(jnp.bfloat16)

def orthonormal(block):
    inner = jnp.dot(block.T, block, precision=lax.Precision.HIGHEST)
    lower = jnp.linalg.cholesky(inner)
    return jax.scipy.linalg.solve_triangular(lower, block.T, lower=True).T

def reference(velocity, snapshot_rank, anchor_index, start_basis):
    vort = lax.map(vorticity, jnp.moveaxis(velocity, 1, 0))
    flat = vort.reshape(M, NCELLS)
    gram = lax.dot_general(flat.astype(jnp.float32), flat.astype(jnp.float32), (((1,), (1,)), ((), ())), preferred_element_type=jnp.float32)
    gram = gram / float(NCELLS)
    scale = jnp.where(snapshot_rank < K, 1.0, 0.25).astype(jnp.float32)
    weighted = scale[:, None] * gram * scale[None, :]
    basis_now = start_basis
    for step in range(ITERS):
        basis_now = orthonormal(jnp.dot(weighted, basis_now, precision=lax.Precision.HIGHEST))
    coef = (scale[:, None] * basis_now).astype(jnp.bfloat16)
    picked = flat[:, anchor_index].astype(jnp.float32)
    anchor = jnp.sum(picked * coef.astype(jnp.float32), axis=0)
    orient = anchor / jnp.maximum(jnp.abs(anchor), 1.0)
    raw = lax.dot_general(coef.astype(jnp.float32), flat.astype(jnp.float32), (((0,), (0,)), ((), ())), preferred_element_type=jnp.float32)
    modes = (raw * orient[:, None]).astype(jnp.bfloat16).reshape(K, P_SIZE, NX, NZ)
    return (modes, basis_now * orient[None, :])
```

```python
import functools
import jax
import jax.numpy as jnp
from jax import lax
from jax.experimental import pallas as pl
from jax.experimental.pallas import tpu as pltpu
from jax.sharding import PartitionSpec as P

ITERS = 3
REACH = 3
MESH = pl.DeviceIdType.MESH
NT = (((1,), (1,)), ((), ()))
F32 = jnp.float32
BF16 = jnp.bfloat16


def iota(shape, dim):
    return lax.broadcasted_iota(jnp.int32, shape, dim)


def stencil_weight(offset):
    size = jnp.abs(offset)
    value = jnp.where(size == 1, 45, jnp.where(size == 2, -9, jnp.where(size == 3, 1, 0)))
    return jnp.where(offset < 0, -value, value).astype(F32).astype(BF16)


def gram_kernel(
    dims, vel_ref, anchor_ref, flat_ref, out_ref,
    wide, uterm, sendx, recvx, sendz, recvz, part, got1, got2, got3,
    sx_sem, rx_sem, sz_sem, rz_sem, s1_sem, r1_sem, s2_sem, r2_sem, s3_sem, r3_sem, s4_sem, r4_sem,
):
    snaps, planes, cx, cz, kept, nx, nz, group = dims
    rows = snaps * planes * cx
    stride = planes * cx
    me_x = lax.axis_index("gx")
    me_z = lax.axis_index("gz")
    member = lax.rem(me_x, group)
    base = me_x - member
    teams = nx // group
    team = me_x // group
    share = part.shape[0] // group
    xnext, xprev = lax.rem(me_x + 1, nx), lax.rem(me_x + nx - 1, nx)
    znext, zprev = lax.rem(me_z + 1, nz), lax.rem(me_z + nz - 1, nz)

    in_group = [(base + lax.rem(member + d, group), me_z) for d in range(1, group)]
    in_teams = [(lax.rem(team + d, teams) * group + member, me_z) for d in range(1, teams)]
    in_z = [(me_x, lax.rem(me_z + d, nz)) for d in range(1, nz)]
    greet = in_group + in_teams + in_z
    if teams > 1:
        greet = greet + [(xnext, me_z), (xprev, me_z)]

    barrier = pltpu.get_barrier_semaphore()
    for peer in greet:
        pl.semaphore_signal(barrier, inc=1, device_id=peer, device_id_type=MESH)

    def remote(src, dst, send, recv, peer):
        return pltpu.make_async_remote_copy(
            src_ref=src, dst_ref=dst, send_sem=send, recv_sem=recv,
            device_id=peer, device_id_type=MESH,
        )

    quarter = rows // 4
    edge = iota((32, cz), 0)
    lane = iota((32, cz), 1)
    packed = jnp.zeros((32, quarter), F32)
    for c in range(4):
        r = edge % 16 - 4 * c
        wanted = jnp.where(edge < 16, cz - REACH + r, r)
        pick = jnp.where((r >= 0) & (r < REACH) & (lane == wanted), 1.0, 0.0).astype(BF16)
        packed = packed + lax.dot_general(
            pick, vel_ref[0, c * quarter : (c + 1) * quarter, :], NT, preferred_element_type=F32
        )
    sendz[...] = packed.astype(BF16).reshape(2, 16, quarter)

    wide[...] = vel_ref[1].astype(F32)
    for p in range(planes):
        for r in range(REACH):
            low = wide[pl.ds(p * cx + r, snaps, stride=stride), :]
            high = wide[pl.ds(p * cx + cx - REACH + r, snaps, stride=stride), :]
            sendx[0, p * REACH + r] = high.astype(BF16)
            sendx[1, p * REACH + r] = low.astype(BF16)

    pl.semaphore_wait(barrier, len(greet))
    halos = [
        remote(sendz.at[0], recvz.at[0], sz_sem.at[0], rz_sem.at[0], (me_x, znext)),
        remote(sendz.at[1], recvz.at[1], sz_sem.at[1], rz_sem.at[1], (me_x, zprev)),
        remote(sendx.at[0], recvx.at[0], sx_sem.at[0], rx_sem.at[0], (xnext, me_z)),
        remote(sendx.at[1], recvx.at[1], sx_sem.at[1], rx_sem.at[1], (xprev, me_z)),
    ]
    for copy in halos:
        copy.start()

    index = anchor_ref[...]
    total_x, total_z = cx * nx, cz * nz
    plane_of = index // (total_x * total_z)
    remain = index % (total_x * total_z)
    local_x = remain // total_z - me_x * cx
    local_z = remain % total_z - me_z * cz
    owned = (local_x >= 0) & (local_x < cx) & (local_z >= 0) & (local_z < cz)
    position = jnp.where(owned, (plane_of * cx + local_x) * cz + local_z, -1).astype(F32)
    column = jnp.transpose(jnp.broadcast_to(position, (kept, kept)))[:, 0:1]

    band = stencil_weight(iota((cz, cz), 1) - iota((cz, cz), 0))
    halos[0].wait_recv()
    halos[1].wait_recv()
    sides = jnp.transpose(recvz[...].reshape(32, quarter).astype(F32)).astype(BF16)
    for c in range(4):
        r = edge % 16 - 4 * c
        source = jnp.where(edge < 16, r - REACH, cz + r)
        valid = (r >= 0) & (r < REACH)
        spread = stencil_weight(jnp.where(valid, lane - source, 0))
        here = slice(c * quarter, (c + 1) * quarter)
        uterm[here, :] = jnp.dot(
            vel_ref[0, here, :], band, preferred_element_type=F32
        ) + jnp.dot(sides, spread, preferred_element_type=F32)
    halos[2].wait_recv()
    halos[3].wait_recv()

    def snapshots(step, carry):
        first = pl.multiple_of(step * 16, 16)
        for p in range(planes):
            layers = []
            for x in range(-REACH, cx + REACH):
                if x < 0:
                    block = recvx[0, p * REACH + x + REACH, pl.ds(first, 16), :].astype(F32)
                elif x >= cx:
                    block = recvx[1, p * REACH + x - cx, pl.ds(first, 16), :].astype(F32)
                else:
                    block = wide[pl.ds(first * stride + p * cx + x, 16, stride=stride), :]
                layers.append(block)
            for x in range(cx):
                at = x + REACH
                value = 45.0 * (layers[at + 1] - layers[at - 1])
                value = value - 9.0 * (layers[at + 2] - layers[at - 2])
                value = value + (layers[at + 3] - layers[at - 3])
                value = value + uterm[pl.ds(first * stride + p * cx + x, 16, stride=stride), :]
                cell = (p * cx + x) * cz
                flat_ref[pl.ds(first, 16), cell : cell + cz] = (value * (1.0 / 60.0)).astype(BF16)
        return carry

    lax.fori_loop(0, snaps // 16, snapshots, 0)

    width = 8 * cz
    cell_in = iota((kept, width), 1).astype(F32)

    def products(step, total):
        at = pl.multiple_of(step * width, width)
        block = flat_ref[:, pl.ds(at, width)]
        mark = jnp.where(cell_in + (step * width).astype(F32) == column, 1.0, 0.0).astype(BF16)
        both = jnp.concatenate([block, mark], axis=0)
        return total + lax.dot_general(both, block, NT, preferred_element_type=F32)

    part[...] = lax.fori_loop(
        0, planes * cx * cz // width, products, jnp.zeros((snaps + kept, snaps), F32)
    )

    started = list(halos)
    first_stage = []
    for d in range(1, group):
        target = lax.rem(member + d, group)
        first_stage.append(remote(
            part.at[pl.ds(target * share, share)], got1.at[d - 1],
            s1_sem.at[d - 1], r1_sem.at[d - 1], in_group[d - 1],
        ))
    for copy in first_stage:
        copy.start()
    mine = part[pl.ds(member * share, share), :]
    for d, copy in enumerate(first_stage):
        copy.wait_recv()
        mine = mine + got1[d]

    def exchange(value, buffer, place, peers, send, recv):
        buffer[place] = value
        copies = [
            remote(buffer.at[place], buffer.at[place], send.at[d], recv.at[d], peer)
            for d, peer in enumerate(peers)
        ]
        for copy in copies:
            copy.start()
        for copy in copies:
            copy.wait_recv()
        started.extend(copies)
        value = buffer[0]
        for other in range(1, len(peers) + 1):
            value = value + buffer[other]
        return value

    if teams > 1:
        mine = exchange(mine, got2, team, in_teams, s4_sem, r4_sem)
    mine = exchange(mine, got3, me_z, in_z, s2_sem, r2_sem)

    home = pl.ds(member * share, share)
    out_ref[home, :] = mine
    last_stage = [
        remote(out_ref.at[home], out_ref.at[home], s3_sem.at[d], r3_sem.at[d], peer)
        for d, peer in enumerate(in_group)
    ]
    for copy in last_stage:
        copy.start()
    for copy in last_stage:
        copy.wait_recv()
    for copy in started + first_stage + last_stage:
        copy.wait_send()


def orthonormal_rows(block, pivots):
    kept, snaps = block.shape
    inner = lax.dot_general(
        block, block, NT, precision=lax.Precision.HIGHEST, preferred_element_type=F32
    )
    groups = kept // 8
    left = [inner[8 * h : 8 * h + 8, :] for h in range(groups)]
    right = [block[8 * h : 8 * h + 8, :] for h in range(groups)]
    row_in = iota((8, snaps), 0)
    for k0 in range(0, kept, pivots):
        g = k0 // 8
        cols = [
            {h: jnp.broadcast_to(left[h][:, k0 + j : k0 + j + 1], (8, snaps)) for h in range(g, groups)}
            for j in range(pivots)
        ]
        for j in range(pivots):
            s = (k0 + j) % 8
            pivot = jnp.broadcast_to(cols[j][g][s : s + 1, :], (8, snaps))
            inverse = 1.0 / pivot
            root = inverse * jnp.sqrt(pivot)
            ahead = [cols[n][g][s : s + 1, :] * inverse for n in range(j + 1, pivots)]
            left_row = left[g][s : s + 1, :] * inverse[:, :kept]
            right_row = right[g][s : s + 1, :] * inverse
            for h in range(g, groups):
                factor = cols[j][h]
                if h == g:
                    factor = jnp.where(row_in > s, factor, 0.0)
                left[h] = left[h] - factor[:, :kept] * left_row
                right[h] = right[h] - factor * right_row
                for n in range(j + 1, pivots):
                    cols[n][h] = cols[n][h] - factor * ahead[n - j - 1]
            right[g] = jnp.where(row_in == s, right[g] * root, right[g])
    return jnp.concatenate(right, axis=0)


def modes_kernel(dims, gram_ref, flat_ref, rank_ref, start_ref, modes_ref, basis_ref, spread):
    snaps, planes, cx, cz, kept, nx, nz, group = dims
    cells = float(planes * cx * nx * cz * nz)
    stride = planes * cx
    scale = jnp.where(rank_ref[...] < kept, 1.0, 0.25).astype(F32)
    down = jnp.transpose(jnp.broadcast_to(scale, (snaps, snaps)))
    weighted = down * (gram_ref[0:snaps, :] / cells) * scale

    def iterate(step, rows):
        moved = lax.dot_general(
            rows, weighted, NT, precision=lax.Precision.HIGHEST, preferred_element_type=F32
        )
        return orthonormal_rows(moved, 4)

    rows = lax.fori_loop(0, ITERS, iterate, jnp.transpose(start_ref[...]))
    coef = (scale * rows).astype(BF16)
    anchor = jnp.sum(gram_ref[snaps : snaps + kept, :] * coef.astype(F32), axis=1, keepdims=True)
    orient = anchor / jnp.maximum(jnp.abs(anchor), 1.0)
    basis_ref[...] = jnp.transpose(rows * orient)
    for block in range(stride):
        raw = jnp.dot(
            coef, flat_ref[:, block * cz : (block + 1) * cz], preferred_element_type=F32
        )
        spread[pl.ds(block, kept, stride=stride), :] = raw * orient
    modes_ref[...] = spread[...].astype(BF16)


def body(nx, nz, velocity, snapshot_rank, anchor_index, start_basis):
    _, snaps, planes, cx, cz = velocity.shape
    kept = start_basis.shape[1]
    total = snaps + kept
    group = max(g for g in (1, 2, 4, 8, 3, 6, 12, 24) if nx % g == 0 and total % (8 * g) == 0)
    dims = (snaps, planes, cx, cz, kept, nx, nz, group)
    rows = snaps * planes * cx
    share = total // group
    teams = nx // group
    vmem = pl.BlockSpec(memory_space=pltpu.VMEM)
    dma = lambda n: pltpu.SemaphoreType.DMA((max(n, 1),))
    flat, gram = pl.pallas_call(
        functools.partial(gram_kernel, dims),
        out_shape=(
            jax.ShapeDtypeStruct((snaps, planes * cx * cz), BF16),
            jax.ShapeDtypeStruct((total, snaps), F32),
        ),
        in_specs=[vmem] * 2,
        out_specs=(vmem, vmem),
        scratch_shapes=[
            pltpu.VMEM((rows, cz), F32),
            pltpu.VMEM((rows, cz), F32),
            pltpu.VMEM((2, planes * REACH, snaps, cz), BF16),
            pltpu.VMEM((2, planes * REACH, snaps, cz), BF16),
            pltpu.VMEM((2, 16, rows // 4), BF16),
            pltpu.VMEM((2, 16, rows // 4), BF16),
            pltpu.VMEM((total, snaps), F32),
            pltpu.VMEM((max(group - 1, 1), share, snaps), F32),
            pltpu.VMEM((teams, share, snaps), F32),
            pltpu.VMEM((nz, share, snaps), F32),
            dma(2), dma(2), dma(2), dma(2),
            dma(group - 1), dma(group - 1),
            dma(nz - 1), dma(nz - 1),
            dma(group - 1), dma(group - 1),
            dma(teams - 1), dma(teams - 1),
        ],
        compiler_params=pltpu.CompilerParams(
            collective_id=0, has_side_effects=True, vmem_limit_bytes=40 * 1024 * 1024
        ),
        name="vorticity_gram",
    )(velocity.reshape(2, rows, cz), anchor_index.reshape(1, kept))
    modes, basis = pl.pallas_call(
        functools.partial(modes_kernel, dims),
        out_shape=(
            jax.ShapeDtypeStruct((kept * planes * cx, cz), BF16),
            jax.ShapeDtypeStruct((snaps, kept), F32),
        ),
        in_specs=[vmem] * 4,
        out_specs=(vmem, vmem),
        scratch_shapes=[pltpu.VMEM((kept * planes * cx, cz), F32)],
        compiler_params=pltpu.CompilerParams(vmem_limit_bytes=40 * 1024 * 1024),
        name="subspace_modes",
    )(gram, flat, snapshot_rank.reshape(1, snaps), start_basis)
    return modes.reshape(kept, planes, cx, cz), basis


def solution(mesh):
    return jax.shard_map(
        functools.partial(body, mesh.shape["gx"], mesh.shape["gz"]),
        mesh=mesh,
        in_specs=(P(None, None, None, "gx", "gz"), P(), P(), P()),
        out_specs=(P(None, None, "gx", "gz"), P()),
        check_vma=False,
    )
```

```python
import functools
import jax
import jax.numpy as jnp
from jax import lax
from jax.experimental import pallas as pl
from jax.experimental.pallas import tpu as pltpu
from jax.sharding import PartitionSpec as P

ITERS = 3
REACH = 3
MESH = pl.DeviceIdType.MESH
NT = (((1,), (1,)), ((), ()))
F32 = jnp.float32
BF16 = jnp.bfloat16


def iota(shape, dim):
    return lax.broadcasted_iota(jnp.int32, shape, dim)


def stencil_weight(offset):
    size = jnp.abs(offset)
    value = jnp.where(size == 1, 45, jnp.where(size == 2, -9, jnp.where(size == 3, 1, 0)))
    return jnp.where(offset < 0, -value, value).astype(F32).astype(BF16)


def gram_kernel(
    dims, vel_ref, anchor_ref, kept_ref, out_ref,
    flat_ref, spans, streams, spots, wide, uterm, sendx, recvx, sendz, recvz, part, got1, got2, got3,
    sx_sem, rx_sem, sz_sem, rz_sem, s1_sem, r1_sem, s2_sem, r2_sem, s3_sem, r3_sem, s4_sem, r4_sem, load_sem,
):
    snaps, planes, cx, cz, kept, nx, nz, group = dims
    rows = snaps * planes * cx
    stride = planes * cx
    me_x = lax.axis_index("gx")
    me_z = lax.axis_index("gz")
    member = lax.rem(me_x, group)
    base = me_x - member
    teams = nx // group
    team = me_x // group
    share = part.shape[0] // group
    xnext, xprev = lax.rem(me_x + 1, nx), lax.rem(me_x + nx - 1, nx)
    znext, zprev = lax.rem(me_z + 1, nz), lax.rem(me_z + nz - 1, nz)

    in_group = [(base + lax.rem(member + d, group), me_z) for d in range(1, group)]
    in_teams = [(lax.rem(team + d, teams) * group + member, me_z) for d in range(1, teams)]
    in_z = [(me_x, lax.rem(me_z + d, nz)) for d in range(1, nz)]
    greet = in_group + in_teams + in_z
    if teams > 1:
        greet = greet + [(xnext, me_z), (xprev, me_z)]

    quarter = rows // 4
    loads = []
    for half, kept_in in ((0, spans), (1, streams)):
        for c in range(4):
            here = pl.ds(c * quarter, quarter)
            loads.append(pltpu.make_async_copy(
                vel_ref.at[half, here], kept_in.at[here], load_sem.at[half * 4 + c]
            ))
    loads.append(pltpu.make_async_copy(anchor_ref, spots, load_sem.at[8]))
    barrier = pltpu.get_barrier_semaphore()
    for peer in greet:
        pl.semaphore_signal(barrier, inc=1, device_id=peer, device_id_type=MESH)
    for copy in loads:
        copy.start()

    def remote(src, dst, send, recv, peer):
        return pltpu.make_async_remote_copy(
            src_ref=src, dst_ref=dst, send_sem=send, recv_sem=recv,
            device_id=peer, device_id_type=MESH,
        )

    edge = iota((32, cz), 0)
    lane = iota((32, cz), 1)
    packed = jnp.zeros((32, quarter), F32)
    for c in range(4):
        r = edge % 16 - 4 * c
        wanted = jnp.where(edge < 16, cz - REACH + r, r)
        pick = jnp.where((r >= 0) & (r < REACH) & (lane == wanted), 1.0, 0.0).astype(BF16)
        loads[c].wait()
        packed = packed + lax.dot_general(
            pick, spans[c * quarter : (c + 1) * quarter, :], NT, preferred_element_type=F32
        )
    sendz[...] = packed.astype(BF16).reshape(2, 16, quarter)
    pl.semaphore_wait(barrier, len(greet))
    halos = [
        remote(sendz.at[0], recvz.at[0], sz_sem.at[0], rz_sem.at[0], (me_x, znext)),
        remote(sendz.at[1], recvz.at[1], sz_sem.at[1], rz_sem.at[1], (me_x, zprev)),
        remote(sendx.at[0], recvx.at[0], sx_sem.at[0], rx_sem.at[0], (xnext, me_z)),
        remote(sendx.at[1], recvx.at[1], sx_sem.at[1], rx_sem.at[1], (xprev, me_z)),
    ]
    halos[0].start()
    halos[1].start()

    some = snaps // 4
    for c in range(4):
        loads[4 + c].wait()
        here = slice(c * quarter, (c + 1) * quarter)
        wide[here, :] = streams[here, :].astype(F32)
        for p in range(planes):
            for r in range(REACH):
                low = c * quarter + p * cx + r
                block = wide[pl.ds(low + cx - REACH, some, stride=stride), :]
                sendx[0, p * REACH + r, c * some : (c + 1) * some, :] = block.astype(BF16)
                block = wide[pl.ds(low, some, stride=stride), :]
                sendx[1, p * REACH + r, c * some : (c + 1) * some, :] = block.astype(BF16)
    halos[2].start()
    halos[3].start()

    loads[8].wait()
    index = spots[...]
    total_x, total_z = cx * nx, cz * nz
    plane_of = index // (total_x * total_z)
    remain = index % (total_x * total_z)
    local_x = remain // total_z - me_x * cx
    local_z = remain % total_z - me_z * cz
    owned = (local_x >= 0) & (local_x < cx) & (local_z >= 0) & (local_z < cz)
    position = jnp.where(owned, (plane_of * cx + local_x) * cz + local_z, -1).astype(F32)
    column = jnp.transpose(jnp.broadcast_to(position, (kept, kept)))[:, 0:1]

    band = stencil_weight(iota((cz, cz), 1) - iota((cz, cz), 0))
    halos[0].wait_recv()
    halos[1].wait_recv()
    sides = jnp.transpose(recvz[...].reshape(32, quarter).astype(F32)).astype(BF16)
    for c in range(4):
        r = edge % 16 - 4 * c
        source = jnp.where(edge < 16, r - REACH, cz + r)
        valid = (r >= 0) & (r < REACH)
        spread = stencil_weight(jnp.where(valid, lane - source, 0))
        here = slice(c * quarter, (c + 1) * quarter)
        uterm[here, :] = jnp.dot(
            spans[here, :], band, preferred_element_type=F32
        ) + jnp.dot(sides, spread, preferred_element_type=F32)

    def snapshots(begin, end):
        def some_rows(step, carry):
            first = pl.multiple_of(step * 16, 16)
            for p in range(planes):
                layers = {}
                for x in range(begin - REACH, end + REACH):
                    if x < 0:
                        block = recvx[0, p * REACH + x + REACH, pl.ds(first, 16), :].astype(F32)
                    elif x >= cx:
                        block = recvx[1, p * REACH + x - cx, pl.ds(first, 16), :].astype(F32)
                    else:
                        block = wide[pl.ds(first * stride + p * cx + x, 16, stride=stride), :]
                    layers[x] = block
                for x in range(begin, end):
                    value = 45.0 * (layers[x + 1] - layers[x - 1])
                    value = value - 9.0 * (layers[x + 2] - layers[x - 2])
                    value = value + (layers[x + 3] - layers[x - 3])
                    value = value + uterm[pl.ds(first * stride + p * cx + x, 16, stride=stride), :]
                    cell = (p * cx + x) * cz
                    flat_ref[pl.ds(first, 16), cell : cell + cz] = (value * (1.0 / 60.0)).astype(BF16)
            return carry

        lax.fori_loop(0, snaps // 16, some_rows, 0)

    def products(begin, end):
        total = jnp.zeros((snaps + kept, snaps), F32)
        for p in range(planes):
            cell, width = (p * cx + begin) * cz, (end - begin) * cz
            block = flat_ref[:, cell : cell + width]
            cell_in = iota((kept, width), 1).astype(F32) + float(cell)
            mark = jnp.where(cell_in == column, 1.0, 0.0).astype(BF16)
            both = jnp.concatenate([block, mark], axis=0)
            total = total + lax.dot_general(both, block, NT, preferred_element_type=F32)
        return total

    snapshots(REACH, cx - REACH)
    part[...] = products(REACH, cx - REACH)
    halos[2].wait_recv()
    halos[3].wait_recv()
    snapshots(0, REACH)
    snapshots(cx - REACH, cx)
    store = pltpu.make_async_copy(flat_ref, kept_ref, load_sem.at[9])
    store.start()
    part[...] += products(0, REACH) + products(cx - REACH, cx)

    started = list(halos)
    first_stage = []
    for d in range(1, group):
        target = lax.rem(member + d, group)
        first_stage.append(remote(
            part.at[pl.ds(target * share, share)], got1.at[d - 1],
            s1_sem.at[d - 1], r1_sem.at[d - 1], in_group[d - 1],
        ))
    for copy in first_stage:
        copy.start()
    mine = part[pl.ds(member * share, share), :]
    for d, copy in enumerate(first_stage):
        copy.wait_recv()
        mine = mine + got1[d]

    def exchange(value, buffer, place, peers, send, recv):
        buffer[place] = value
        copies = [
            remote(buffer.at[place], buffer.at[place], send.at[d], recv.at[d], peer)
            for d, peer in enumerate(peers)
        ]
        for copy in copies:
            copy.start()
        for copy in copies:
            copy.wait_recv()
        started.extend(copies)
        value = buffer[0]
        for other in range(1, len(peers) + 1):
            value = value + buffer[other]
        return value

    if teams > 1:
        mine = exchange(mine, got2, team, in_teams, s4_sem, r4_sem)
    mine = exchange(mine, got3, me_z, in_z, s2_sem, r2_sem)

    home = pl.ds(member * share, share)
    out_ref[home, :] = mine
    last_stage = [
        remote(out_ref.at[home], out_ref.at[home], s3_sem.at[d], r3_sem.at[d], peer)
        for d, peer in enumerate(in_group)
    ]
    for copy in last_stage:
        copy.start()
    for copy in last_stage:
        copy.wait_recv()
    for copy in started + first_stage + last_stage:
        copy.wait_send()
    store.wait()


def orthonormal_rows(block, pivots):
    kept, snaps = block.shape
    inner = lax.dot_general(
        block, block, NT, precision=lax.Precision.HIGHEST, preferred_element_type=F32
    )
    groups = kept // 8
    left = [inner[8 * h : 8 * h + 8, :] for h in range(groups)]
    right = [block[8 * h : 8 * h + 8, :] for h in range(groups)]
    row_in = iota((8, snaps), 0)
    for k0 in range(0, kept, pivots):
        g, s0 = k0 // 8, k0 % 8
        ahead = range(pivots)
        cols = [
            [None] * g
            + [jnp.broadcast_to(left[h][:, k0 + n : k0 + n + 1], (8, snaps)) for h in range(g, groups)]
            for n in ahead
        ]
        own = [
            [jnp.broadcast_to(cols[n][g][s0 + j : s0 + j + 1, :], (8, snaps)) for n in ahead]
            for j in ahead
        ]
        lrow = [jnp.broadcast_to(left[g][s0 + j : s0 + j + 1, :], (8, kept)) for j in ahead]
        rrow = [jnp.broadcast_to(right[g][s0 + j : s0 + j + 1, :], (8, snaps)) for j in ahead]
        for j in ahead:
            pivot = own[j][j]
            inverse = 1.0 / pivot
            for n in range(j + 1, pivots):
                for m in range(n, pivots):
                    own[n][m] = own[n][m] - (own[j][n] * own[j][m]) * inverse
            for n in range(j + 1, pivots):
                times = own[j][n] * inverse
                lrow[n] = lrow[n] - times[:, :kept] * lrow[j]
                rrow[n] = rrow[n] - times * rrow[j]
                for h in range(g, groups):
                    cols[n][h] = cols[n][h] - times * cols[j][h]
            for h in range(g, groups):
                factor = cols[j][h] * inverse
                if h == g:
                    factor = jnp.where(row_in > s0 + j, factor, 0.0)
                left[h] = left[h] - factor[:, :kept] * lrow[j]
                right[h] = right[h] - factor * rrow[j]
            right[g] = jnp.where(row_in == s0 + j, rrow[j] * (inverse * jnp.sqrt(pivot)), right[g])
    return jnp.concatenate(right, axis=0)


def modes_kernel(dims, gram_ref, kept_ref, rank_ref, start_ref, modes_ref, basis_ref, flat_ref, spread, sem):
    snaps, planes, cx, cz, kept, nx, nz, group = dims
    fetch = pltpu.make_async_copy(kept_ref, flat_ref, sem)
    fetch.start()
    cells = float(planes * cx * nx * cz * nz)
    stride = planes * cx
    scale = jnp.where(rank_ref[...] < kept, 1.0, 0.25).astype(F32)
    down = jnp.transpose(jnp.broadcast_to(scale, (snaps, snaps)))
    weighted = down * (gram_ref[0:snaps, :] / cells) * scale

    def iterate(step, rows):
        moved = lax.dot_general(
            rows, weighted, NT, precision=lax.Precision.HIGHEST, preferred_element_type=F32
        )
        return orthonormal_rows(moved, 4)

    rows = lax.fori_loop(0, ITERS, iterate, start_ref[...])
    coef = (scale * rows).astype(BF16)
    anchor = jnp.sum(gram_ref[snaps : snaps + kept, :] * coef.astype(F32), axis=1, keepdims=True)
    orient = anchor / jnp.maximum(jnp.abs(anchor), 1.0)
    basis_ref[...] = rows * orient
    fetch.wait()
    for first in range(0, stride, 4):
        raw = orient * jnp.dot(
            coef, flat_ref[:, first * cz : (first + 4) * cz], preferred_element_type=F32
        )
        for n in range(4):
            spread[pl.ds(first + n, kept, stride=stride), :] = raw[:, n * cz : (n + 1) * cz]
    modes_ref[...] = spread[...].astype(BF16)


def body(nx, nz, velocity, snapshot_rank, anchor_index, start_basis):
    _, snaps, planes, cx, cz = velocity.shape
    kept = start_basis.shape[1]
    total = snaps + kept
    group = max(g for g in (1, 2, 4, 8, 3, 6, 12, 24) if nx % g == 0 and total % (8 * g) == 0)
    dims = (snaps, planes, cx, cz, kept, nx, nz, group)
    rows = snaps * planes * cx
    share = total // group
    teams = nx // group
    vmem = pl.BlockSpec(memory_space=pltpu.VMEM)
    hbm = pl.BlockSpec(memory_space=pltpu.HBM)
    dma = lambda n: pltpu.SemaphoreType.DMA((max(n, 1),))
    flat, gram = pl.pallas_call(
        functools.partial(gram_kernel, dims),
        out_shape=(
            jax.ShapeDtypeStruct((snaps, planes * cx * cz), BF16),
            jax.ShapeDtypeStruct((total, snaps), F32),
        ),
        in_specs=[hbm] * 2,
        out_specs=(hbm, vmem),
        scratch_shapes=[
            pltpu.VMEM((snaps, planes * cx * cz), BF16),
            pltpu.VMEM((rows, cz), BF16),
            pltpu.VMEM((rows, cz), BF16),
            pltpu.VMEM((1, kept), jnp.int32),
            pltpu.VMEM((rows, cz), F32),
            pltpu.VMEM((rows, cz), F32),
            pltpu.VMEM((2, planes * REACH, snaps, cz), BF16),
            pltpu.VMEM((2, planes * REACH, snaps, cz), BF16),
            pltpu.VMEM((2, 16, rows // 4), BF16),
            pltpu.VMEM((2, 16, rows // 4), BF16),
            pltpu.VMEM((total, snaps), F32),
            pltpu.VMEM((max(group - 1, 1), share, snaps), F32),
            pltpu.VMEM((teams, share, snaps), F32),
            pltpu.VMEM((nz, share, snaps), F32),
            dma(2), dma(2), dma(2), dma(2),
            dma(group - 1), dma(group - 1),
            dma(nz - 1), dma(nz - 1),
            dma(group - 1), dma(group - 1),
            dma(teams - 1), dma(teams - 1), dma(10),
        ],
        compiler_params=pltpu.CompilerParams(
            collective_id=0, has_side_effects=True, vmem_limit_bytes=58 * 1024 * 1024
        ),
        name="vorticity_gram",
    )(velocity.reshape(2, rows, cz), anchor_index.reshape(1, kept))
    modes, basis = pl.pallas_call(
        functools.partial(modes_kernel, dims),
        out_shape=(
            jax.ShapeDtypeStruct((kept * planes * cx, cz), BF16),
            jax.ShapeDtypeStruct((kept, snaps), F32),
        ),
        in_specs=[vmem, hbm, vmem, vmem],
        out_specs=(vmem, vmem),
        scratch_shapes=[
            pltpu.VMEM((snaps, planes * cx * cz), BF16),
            pltpu.VMEM((kept * planes * cx, cz), F32),
            pltpu.SemaphoreType.DMA,
        ],
        compiler_params=pltpu.CompilerParams(vmem_limit_bytes=58 * 1024 * 1024),
        name="subspace_modes",
    )(gram, flat, snapshot_rank.reshape(1, snaps), start_basis.T)
    return modes.reshape(kept, planes, cx, cz), basis.T


def solution(mesh):
    return jax.shard_map(
        functools.partial(body, mesh.shape["gx"], mesh.shape["gz"]),
        mesh=mesh,
        in_specs=(P(None, None, None, "gx", "gz"), P(), P(), P()),
        out_specs=(P(None, None, "gx", "gz"), P()),
        check_vma=False,
    )
```

```python
import functools
import jax
import jax.numpy as jnp
from jax import lax
from jax.experimental import pallas as pl
from jax.experimental.pallas import tpu as pltpu
from jax.sharding import PartitionSpec as P

ITERS = 3
REACH = 3
MESH = pl.DeviceIdType.MESH
NT = (((1,), (1,)), ((), ()))
F32 = jnp.float32
BF16 = jnp.bfloat16


def iota(shape, dim):
    return lax.broadcasted_iota(jnp.int32, shape, dim)


def stencil_weight(offset):
    size = jnp.abs(offset)
    value = jnp.where(size == 1, 45, jnp.where(size == 2, -9, jnp.where(size == 3, 1, 0)))
    return jnp.where(offset < 0, -value, value).astype(F32).astype(BF16)


def gram_kernel(
    dims, vel_ref, anchor_ref, kept_ref, out_ref,
    flat_ref, spans, streams, spots, wide, uterm, sendx, recvx, sendz, recvz, part, got1, got2, got3,
    sx_sem, rx_sem, sz_sem, rz_sem, s1_sem, r1_sem, s2_sem, r2_sem, s3_sem, r3_sem, s4_sem, r4_sem, load_sem,
):
    snaps, planes, cx, cz, kept, nx, nz, group = dims
    rows = snaps * planes * cx
    stride = planes * cx
    pitch = stride + 1
    me_x = lax.axis_index("gx")
    me_z = lax.axis_index("gz")
    member = lax.rem(me_x, group)
    base = me_x - member
    teams = nx // group
    team = me_x // group
    share = part.shape[0] // group
    xnext, xprev = lax.rem(me_x + 1, nx), lax.rem(me_x + nx - 1, nx)
    znext, zprev = lax.rem(me_z + 1, nz), lax.rem(me_z + nz - 1, nz)

    in_group = [(base + lax.rem(member + d, group), me_z) for d in range(1, group)]
    in_teams = [(lax.rem(team + d, teams) * group + member, me_z) for d in range(1, teams)]
    in_z = [(me_x, lax.rem(me_z + d, nz)) for d in range(1, nz)]
    greet = in_group + in_teams + in_z
    if teams > 1:
        greet = greet + [(xnext, me_z), (xprev, me_z)]

    quarter = rows // 4
    loads = []
    for half, kept_in in ((0, spans), (1, streams)):
        for c in range(4):
            here = pl.ds(c * quarter, quarter)
            loads.append(pltpu.make_async_copy(
                vel_ref.at[half, here], kept_in.at[here], load_sem.at[half * 4 + c]
            ))
    loads.append(pltpu.make_async_copy(anchor_ref, spots, load_sem.at[8]))
    barrier = pltpu.get_barrier_semaphore()
    for peer in greet:
        pl.semaphore_signal(barrier, inc=1, device_id=peer, device_id_type=MESH)
    for copy in loads:
        copy.start()

    def remote(src, dst, send, recv, peer):
        return pltpu.make_async_remote_copy(
            src_ref=src, dst_ref=dst, send_sem=send, recv_sem=recv,
            device_id=peer, device_id_type=MESH,
        )

    edge = iota((32, cz), 0)
    lane = iota((32, cz), 1)
    packed = jnp.zeros((32, quarter), F32)
    for c in range(4):
        r = edge % 16 - 4 * c
        wanted = jnp.where(edge < 16, cz - REACH + r, r)
        pick = jnp.where((r >= 0) & (r < REACH) & (lane == wanted), 1.0, 0.0).astype(BF16)
        loads[c].wait()
        packed = packed + lax.dot_general(
            pick, spans[c * quarter : (c + 1) * quarter, :], NT, preferred_element_type=F32
        )
    sendz[...] = packed.astype(BF16).reshape(2, 16, quarter)
    pl.semaphore_wait(barrier, len(greet))
    halos = [
        remote(sendz.at[0], recvz.at[0], sz_sem.at[0], rz_sem.at[0], (me_x, znext)),
        remote(sendz.at[1], recvz.at[1], sz_sem.at[1], rz_sem.at[1], (me_x, zprev)),
        remote(sendx.at[0], recvx.at[0], sx_sem.at[0], rx_sem.at[0], (xnext, me_z)),
        remote(sendx.at[1], recvx.at[1], sx_sem.at[1], rx_sem.at[1], (xprev, me_z)),
    ]
    halos[0].start()
    halos[1].start()

    some = snaps // 4
    for c in range(4):
        loads[4 + c].wait()

        def widen(m, carry, first=c * some):
            at = pl.multiple_of((first + m) * stride, 16)
            wide[pl.ds((first + m) * pitch, stride), :] = streams[pl.ds(at, stride), :].astype(F32)
            return carry

        lax.fori_loop(0, some, widen, 0, unroll=8)
        for p in range(planes):
            for r in range(REACH):
                low = c * some * pitch + p * cx + r
                block = wide[pl.ds(low + cx - REACH, some, stride=pitch), :]
                sendx[0, p * REACH + r, c * some : (c + 1) * some, :] = block.astype(BF16)
                block = wide[pl.ds(low, some, stride=pitch), :]
                sendx[1, p * REACH + r, c * some : (c + 1) * some, :] = block.astype(BF16)
    halos[2].start()
    halos[3].start()

    loads[8].wait()
    index = spots[...]
    total_x, total_z = cx * nx, cz * nz
    plane_of = index // (total_x * total_z)
    remain = index % (total_x * total_z)
    local_x = remain // total_z - me_x * cx
    local_z = remain % total_z - me_z * cz
    owned = (local_x >= 0) & (local_x < cx) & (local_z >= 0) & (local_z < cz)
    position = jnp.where(owned, (plane_of * cx + local_x) * cz + local_z, -1).astype(F32)
    column = jnp.transpose(jnp.broadcast_to(position, (kept, kept)))[:, 0:1]

    band = stencil_weight(iota((cz, cz), 1) - iota((cz, cz), 0))
    halos[0].wait_recv()
    halos[1].wait_recv()
    sides = jnp.transpose(recvz[...].reshape(32, quarter).astype(F32)).astype(BF16)

    def spanwise(c, carry):
        r = edge % 16 - 4 * c
        source = jnp.where(edge < 16, r - REACH, cz + r)
        valid = (r >= 0) & (r < REACH)
        spread = stencil_weight(jnp.where(valid, lane - source, 0))
        here = pl.ds(pl.multiple_of(c * quarter, 16), quarter)
        value = jnp.dot(
            spans[here, :], band, preferred_element_type=F32
        ) + jnp.dot(sides, spread, preferred_element_type=F32)
        for m in range(some):
            at = pl.ds((c * some + m) * pitch, stride)
            uterm[at, :] = value[m * stride : (m + 1) * stride, :]
        return carry

    lax.fori_loop(0, 4, spanwise, 0)

    def snapshots(begin, end):
        def some_rows(step, carry):
            first = pl.multiple_of(step * 16, 16)
            for p in range(planes):
                layers = {}
                for x in range(begin - REACH, end + REACH):
                    if x < 0:
                        block = recvx[0, p * REACH + x + REACH, pl.ds(first, 16), :].astype(F32)
                    elif x >= cx:
                        block = recvx[1, p * REACH + x - cx, pl.ds(first, 16), :].astype(F32)
                    else:
                        block = wide[pl.ds(first * pitch + p * cx + x, 16, stride=pitch), :]
                    layers[x] = block
                for x in range(begin, end):
                    value = 45.0 * (layers[x + 1] - layers[x - 1])
                    value = value - 9.0 * (layers[x + 2] - layers[x - 2])
                    value = value + (layers[x + 3] - layers[x - 3])
                    value = value + uterm[pl.ds(first * pitch + p * cx + x, 16, stride=pitch), :]
                    cell = (p * cx + x) * cz
                    flat_ref[pl.ds(first, 16), cell : cell + cz] = (value * (1.0 / 60.0)).astype(BF16)
            return carry

        lax.fori_loop(0, snaps // 16, some_rows, 0)

    def products(begin, end):
        total = jnp.zeros((snaps + kept, snaps), F32)
        for p in range(planes):
            cell, width = (p * cx + begin) * cz, (end - begin) * cz
            block = flat_ref[:, cell : cell + width]
            cell_in = iota((kept, width), 1).astype(F32) + float(cell)
            mark = jnp.where(cell_in == column, 1.0, 0.0).astype(BF16)
            both = jnp.concatenate([block, mark], axis=0)
            total = total + lax.dot_general(both, block, NT, preferred_element_type=F32)
        return total

    snapshots(REACH, cx - REACH)
    part[...] = products(REACH, cx - REACH)
    halos[2].wait_recv()
    halos[3].wait_recv()
    snapshots(0, REACH)
    snapshots(cx - REACH, cx)
    store = pltpu.make_async_copy(flat_ref, kept_ref, load_sem.at[9])
    store.start()
    part[...] += products(0, REACH) + products(cx - REACH, cx)

    started = list(halos)
    first_stage = []
    for d in range(1, group):
        target = lax.rem(member + d, group)
        first_stage.append(remote(
            part.at[pl.ds(target * share, share)], got1.at[d - 1],
            s1_sem.at[d - 1], r1_sem.at[d - 1], in_group[d - 1],
        ))
    for copy in first_stage:
        copy.start()
    mine = part[pl.ds(member * share, share), :]
    for d, copy in enumerate(first_stage):
        copy.wait_recv()
        mine = mine + got1[d]

    def exchange(value, buffer, place, peers, send, recv):
        buffer[place] = value
        copies = [
            remote(buffer.at[place], buffer.at[place], send.at[d], recv.at[d], peer)
            for d, peer in enumerate(peers)
        ]
        for copy in copies:
            copy.start()
        for copy in copies:
            copy.wait_recv()
        started.extend(copies)
        value = buffer[0]
        for other in range(1, len(peers) + 1):
            value = value + buffer[other]
        return value

    if teams > 1:
        mine = exchange(mine, got2, team, in_teams, s4_sem, r4_sem)
    mine = exchange(mine, got3, me_z, in_z, s2_sem, r2_sem)

    home = pl.ds(member * share, share)
    out_ref[home, :] = mine
    last_stage = [
        remote(out_ref.at[home], out_ref.at[home], s3_sem.at[d], r3_sem.at[d], peer)
        for d, peer in enumerate(in_group)
    ]
    for copy in last_stage:
        copy.start()
    for copy in last_stage:
        copy.wait_recv()
    for copy in started + first_stage + last_stage:
        copy.wait_send()
    store.wait()


def orthonormal_rows(block, pivots):
    kept, snaps = block.shape
    inner = lax.dot_general(
        block, block, NT, precision=lax.Precision.HIGHEST, preferred_element_type=F32
    )
    groups = kept // 8
    left = [inner[8 * h : 8 * h + 8, :] for h in range(groups)]
    right = [block[8 * h : 8 * h + 8, :] for h in range(groups)]
    row_in = iota((8, snaps), 0)
    for k0 in range(0, kept, pivots):
        g, s0 = k0 // 8, k0 % 8
        ahead = range(pivots)
        cols = [
            [None] * g
            + [jnp.broadcast_to(left[h][:, k0 + n : k0 + n + 1], (8, snaps)) for h in range(g, groups)]
            for n in ahead
        ]
        own = [
            [jnp.broadcast_to(cols[n][g][s0 + j : s0 + j + 1, :], (8, snaps)) for n in ahead]
            for j in ahead
        ]
        lrow = [jnp.broadcast_to(left[g][s0 + j : s0 + j + 1, :], (8, kept)) for j in ahead]
        rrow = [jnp.broadcast_to(right[g][s0 + j : s0 + j + 1, :], (8, snaps)) for j in ahead]
        for j in ahead:
            pivot = own[j][j]
            inverse = 1.0 / pivot
            for n in range(j + 1, pivots):
                for m in range(n, pivots):
                    own[n][m] = own[n][m] - (own[j][n] * own[j][m]) * inverse
            for n in range(j + 1, pivots):
                times = own[j][n] * inverse
                lrow[n] = lrow[n] - times[:, :kept] * lrow[j]
                rrow[n] = rrow[n] - times * rrow[j]
                for h in range(g, groups):
                    cols[n][h] = cols[n][h] - times * cols[j][h]
            for h in range(g, groups):
                factor = cols[j][h] * inverse
                if h == g:
                    factor = jnp.where(row_in > s0 + j, factor, 0.0)
                left[h] = left[h] - factor[:, :kept] * lrow[j]
                right[h] = right[h] - factor * rrow[j]
            right[g] = jnp.where(row_in == s0 + j, rrow[j] * (inverse * jnp.sqrt(pivot)), right[g])
    return jnp.concatenate(right, axis=0)


def modes_kernel(dims, gram_ref, kept_ref, rank_ref, start_ref, modes_ref, basis_ref, flat_ref, spread, sem):
    snaps, planes, cx, cz, kept, nx, nz, group = dims
    fetch = pltpu.make_async_copy(kept_ref, flat_ref, sem)
    fetch.start()
    cells = float(planes * cx * nx * cz * nz)
    stride = planes * cx
    scale = jnp.where(rank_ref[...] < kept, 1.0, 0.25).astype(F32)
    down = jnp.transpose(jnp.broadcast_to(scale, (snaps, snaps)))
    weighted = down * (gram_ref[0:snaps, :] / cells) * scale

    def iterate(step, rows):
        moved = lax.dot_general(
            rows, weighted, NT, precision=lax.Precision.HIGHEST, preferred_element_type=F32
        )
        return orthonormal_rows(moved, 4)

    rows = lax.fori_loop(0, ITERS, iterate, start_ref[...])
    coef = (scale * rows).astype(BF16)
    anchor = jnp.sum(gram_ref[snaps : snaps + kept, :] * coef.astype(F32), axis=1, keepdims=True)
    orient = anchor / jnp.maximum(jnp.abs(anchor), 1.0)
    basis_ref[...] = rows * orient
    fetch.wait()
    for first in range(0, stride, 4):
        raw = orient * jnp.dot(
            coef, flat_ref[:, first * cz : (first + 4) * cz], preferred_element_type=F32
        )
        for n in range(4):
            spread[pl.ds(first + n, kept, stride=stride + 1), :] = raw[:, n * cz : (n + 1) * cz]

    def narrow(k, carry):
        block = spread[pl.ds(k * (stride + 1), stride), :]
        modes_ref[pl.ds(pl.multiple_of(k * stride, 16), stride), :] = block.astype(BF16)
        return carry

    lax.fori_loop(0, kept, narrow, 0, unroll=8)


def body(nx, nz, velocity, snapshot_rank, anchor_index, start_basis):
    _, snaps, planes, cx, cz = velocity.shape
    kept = start_basis.shape[1]
    total = snaps + kept
    group = max(g for g in (1, 2, 4, 8, 3, 6, 12, 24) if nx % g == 0 and total % (8 * g) == 0)
    dims = (snaps, planes, cx, cz, kept, nx, nz, group)
    rows = snaps * planes * cx
    share = total // group
    teams = nx // group
    vmem = pl.BlockSpec(memory_space=pltpu.VMEM)
    hbm = pl.BlockSpec(memory_space=pltpu.HBM)
    dma = lambda n: pltpu.SemaphoreType.DMA((max(n, 1),))
    flat, gram = pl.pallas_call(
        functools.partial(gram_kernel, dims),
        out_shape=(
            jax.ShapeDtypeStruct((snaps, planes * cx * cz), BF16),
            jax.ShapeDtypeStruct((total, snaps), F32),
        ),
        in_specs=[hbm] * 2,
        out_specs=(hbm, vmem),
        scratch_shapes=[
            pltpu.VMEM((snaps, planes * cx * cz), BF16),
            pltpu.VMEM((rows, cz), BF16),
            pltpu.VMEM((rows, cz), BF16),
            pltpu.VMEM((1, kept), jnp.int32),
            pltpu.VMEM((rows + snaps, cz), F32),
            pltpu.VMEM((rows + snaps, cz), F32),
            pltpu.VMEM((2, planes * REACH, snaps, cz), BF16),
            pltpu.VMEM((2, planes * REACH, snaps, cz), BF16),
            pltpu.VMEM((2, 16, rows // 4), BF16),
            pltpu.VMEM((2, 16, rows // 4), BF16),
            pltpu.VMEM((total, snaps), F32),
            pltpu.VMEM((max(group - 1, 1), share, snaps), F32),
            pltpu.VMEM((teams, share, snaps), F32),
            pltpu.VMEM((nz, share, snaps), F32),
            dma(2), dma(2), dma(2), dma(2),
            dma(group - 1), dma(group - 1),
            dma(nz - 1), dma(nz - 1),
            dma(group - 1), dma(group - 1),
            dma(teams - 1), dma(teams - 1), dma(10),
        ],
        compiler_params=pltpu.CompilerParams(
            collective_id=0, has_side_effects=True, vmem_limit_bytes=58 * 1024 * 1024
        ),
        name="vorticity_gram",
    )(velocity.reshape(2, rows, cz), anchor_index.reshape(1, kept))
    modes, basis = pl.pallas_call(
        functools.partial(modes_kernel, dims),
        out_shape=(
            jax.ShapeDtypeStruct((kept * planes * cx, cz), BF16),
            jax.ShapeDtypeStruct((kept, snaps), F32),
        ),
        in_specs=[vmem, hbm, vmem, vmem],
        out_specs=(vmem, vmem),
        scratch_shapes=[
            pltpu.VMEM((snaps, planes * cx * cz), BF16),
            pltpu.VMEM((kept * (planes * cx + 1), cz), F32),
            pltpu.SemaphoreType.DMA,
        ],
        compiler_params=pltpu.CompilerParams(vmem_limit_bytes=58 * 1024 * 1024),
        name="subspace_modes",
    )(gram, flat, snapshot_rank.reshape(1, snaps), start_basis.T)
    return modes.reshape(kept, planes, cx, cz), basis.T


def solution(mesh):
    return jax.shard_map(
        functools.partial(body, mesh.shape["gx"], mesh.shape["gz"]),
        mesh=mesh,
        in_specs=(P(None, None, None, "gx", "gz"), P(), P(), P()),
        out_specs=(P(None, None, "gx", "gz"), P()),
        check_vma=False,
    )
```

```python
import functools
import jax
import jax.numpy as jnp
from jax import lax
from jax.experimental import pallas as pl
from jax.experimental.pallas import tpu as pltpu
from jax.sharding import PartitionSpec as P

ITERS = 3
REACH = 3
MESH = pl.DeviceIdType.MESH
NT = (((1,), (1,)), ((), ()))
F32 = jnp.float32
BF16 = jnp.bfloat16


def iota(shape, dim):
    return lax.broadcasted_iota(jnp.int32, shape, dim)


def stencil_weight(offset):
    size = jnp.abs(offset)
    value = jnp.where(size == 1, 45, jnp.where(size == 2, -9, jnp.where(size == 3, 1, 0)))
    return jnp.where(offset < 0, -value, value).astype(F32).astype(BF16)


def gram_kernel(
    dims, vel_ref, anchor_ref, kept_ref, out_ref,
    flat_ref, spans, streams, spots, wide, uterm, sendx, recvx, sendz, recvz, part, got1, got2, got3,
    sx_sem, rx_sem, sz_sem, rz_sem, s1_sem, r1_sem, s2_sem, r2_sem, s3_sem, r3_sem, s4_sem, r4_sem, load_sem,
):
    snaps, planes, cx, cz, kept, nx, nz, group = dims
    rows = snaps * planes * cx
    stride = planes * cx
    pitch = stride + 1
    me_x = lax.axis_index("gx")
    me_z = lax.axis_index("gz")
    member = lax.rem(me_x, group)
    base = me_x - member
    teams = nx // group
    team = me_x // group
    share = part.shape[0] // group
    xnext, xprev = lax.rem(me_x + 1, nx), lax.rem(me_x + nx - 1, nx)
    znext, zprev = lax.rem(me_z + 1, nz), lax.rem(me_z + nz - 1, nz)

    in_group = [(base + lax.rem(member + d, group), me_z) for d in range(1, group)]
    in_teams = [(lax.rem(team + d, teams) * group + member, me_z) for d in range(1, teams)]
    in_z = [(me_x, lax.rem(me_z + d, nz)) for d in range(1, nz)]
    greet = in_group + in_teams + in_z
    if teams > 1:
        greet = greet + [(xnext, me_z), (xprev, me_z)]

    quarter = rows // 4
    loads = []
    for half, kept_in in ((0, spans), (1, streams)):
        for c in range(4):
            here = pl.ds(c * quarter, quarter)
            loads.append(pltpu.make_async_copy(
                vel_ref.at[half, here], kept_in.at[here], load_sem.at[half * 4 + c]
            ))
    loads.append(pltpu.make_async_copy(anchor_ref, spots, load_sem.at[8]))
    barrier = pltpu.get_barrier_semaphore()
    for peer in greet:
        pl.semaphore_signal(barrier, inc=1, device_id=peer, device_id_type=MESH)
    for copy in loads:
        copy.start()

    def remote(src, dst, send, recv, peer):
        return pltpu.make_async_remote_copy(
            src_ref=src, dst_ref=dst, send_sem=send, recv_sem=recv,
            device_id=peer, device_id_type=MESH,
        )

    edge = iota((32, cz), 0)
    lane = iota((32, cz), 1)
    packed = jnp.zeros((32, quarter), F32)
    for c in range(4):
        r = edge % 16 - 4 * c
        wanted = jnp.where(edge < 16, cz - REACH + r, r)
        pick = jnp.where((r >= 0) & (r < REACH) & (lane == wanted), 1.0, 0.0).astype(BF16)
        loads[c].wait()
        packed = packed + lax.dot_general(
            pick, spans[c * quarter : (c + 1) * quarter, :], NT, preferred_element_type=F32
        )
    sendz[...] = packed.astype(BF16).reshape(2, 16, quarter)
    pl.semaphore_wait(barrier, len(greet))
    halos = [
        remote(sendz.at[0], recvz.at[0], sz_sem.at[0], rz_sem.at[0], (me_x, znext)),
        remote(sendz.at[1], recvz.at[1], sz_sem.at[1], rz_sem.at[1], (me_x, zprev)),
        remote(sendx.at[0], recvx.at[0], sx_sem.at[0], rx_sem.at[0], (xnext, me_z)),
        remote(sendx.at[1], recvx.at[1], sx_sem.at[1], rx_sem.at[1], (xprev, me_z)),
    ]
    halos[0].start()
    halos[1].start()

    some = snaps // 4
    for c in range(4):
        loads[4 + c].wait()

        def widen(m, carry, first=c * some):
            at = pl.multiple_of((first + m) * stride, 16)
            wide[pl.ds((first + m) * pitch, stride), :] = streams[pl.ds(at, stride), :].astype(F32)
            return carry

        lax.fori_loop(0, some, widen, 0, unroll=8)
        for p in range(planes):
            for r in range(REACH):
                low = c * some * pitch + p * cx + r
                block = wide[pl.ds(low + cx - REACH, some, stride=pitch), :]
                sendx[0, p * REACH + r, c * some : (c + 1) * some, :] = block.astype(BF16)
                block = wide[pl.ds(low, some, stride=pitch), :]
                sendx[1, p * REACH + r, c * some : (c + 1) * some, :] = block.astype(BF16)
    halos[2].start()
    halos[3].start()

    loads[8].wait()
    index = spots[...]
    total_x, total_z = cx * nx, cz * nz
    plane_of = index // (total_x * total_z)
    remain = index % (total_x * total_z)
    local_x = remain // total_z - me_x * cx
    local_z = remain % total_z - me_z * cz
    owned = (local_x >= 0) & (local_x < cx) & (local_z >= 0) & (local_z < cz)
    position = jnp.where(owned, (plane_of * cx + local_x) * cz + local_z, -1).astype(F32)
    column = jnp.transpose(jnp.broadcast_to(position, (kept, kept)))[:, 0:1]

    band = stencil_weight(iota((cz, cz), 1) - iota((cz, cz), 0))
    halos[0].wait_recv()
    halos[1].wait_recv()
    sides = jnp.transpose(recvz[...].reshape(32, quarter).astype(F32)).astype(BF16)

    def spanwise(c, carry):
        r = edge % 16 - 4 * c
        source = jnp.where(edge < 16, r - REACH, cz + r)
        valid = (r >= 0) & (r < REACH)
        spread = stencil_weight(jnp.where(valid, lane - source, 0))
        here = pl.ds(pl.multiple_of(c * quarter, 16), quarter)
        value = jnp.dot(
            spans[here, :], band, preferred_element_type=F32
        ) + jnp.dot(sides, spread, preferred_element_type=F32)
        for m in range(some):
            at = pl.ds((c * some + m) * pitch, stride)
            uterm[at, :] = value[m * stride : (m + 1) * stride, :]
        return carry

    lax.fori_loop(0, 4, spanwise, 0)

    def snapshots(begin, end):
        def some_rows(step, carry):
            first = pl.multiple_of(step * 16, 16)
            for p in range(planes):
                layers = {}
                for x in range(begin - REACH, end + REACH):
                    if x < 0:
                        block = recvx[0, p * REACH + x + REACH, pl.ds(first, 16), :].astype(F32)
                    elif x >= cx:
                        block = recvx[1, p * REACH + x - cx, pl.ds(first, 16), :].astype(F32)
                    else:
                        block = wide[pl.ds(first * pitch + p * cx + x, 16, stride=pitch), :]
                    layers[x] = block
                for x in range(begin, end):
                    value = 45.0 * (layers[x + 1] - layers[x - 1])
                    value = value - 9.0 * (layers[x + 2] - layers[x - 2])
                    value = value + (layers[x + 3] - layers[x - 3])
                    value = value + uterm[pl.ds(first * pitch + p * cx + x, 16, stride=pitch), :]
                    cell = (p * cx + x) * cz
                    flat_ref[pl.ds(first, 16), cell : cell + cz] = (value * (1.0 / 60.0)).astype(BF16)
            return carry

        lax.fori_loop(0, snaps // 16, some_rows, 0)

    def products(begin, end):
        total = jnp.zeros((snaps + kept, snaps), F32)
        for p in range(planes):
            cell, width = (p * cx + begin) * cz, (end - begin) * cz
            block = flat_ref[:, cell : cell + width]
            cell_in = iota((kept, width), 1).astype(F32) + float(cell)
            mark = jnp.where(cell_in == column, 1.0, 0.0).astype(BF16)
            both = jnp.concatenate([block, mark], axis=0)
            total = total + lax.dot_general(both, block, NT, preferred_element_type=F32)
        return total

    snapshots(REACH, cx - REACH)
    part[...] = products(REACH, cx - REACH)
    halos[2].wait_recv()
    halos[3].wait_recv()
    snapshots(0, REACH)
    snapshots(cx - REACH, cx)
    store = pltpu.make_async_copy(flat_ref, kept_ref, load_sem.at[9])
    store.start()
    part[...] += products(0, REACH) + products(cx - REACH, cx)

    started = list(halos)
    first_stage = []
    for d in range(1, group):
        target = lax.rem(member + d, group)
        first_stage.append(remote(
            part.at[pl.ds(target * share, share)], got1.at[d - 1],
            s1_sem.at[d - 1], r1_sem.at[d - 1], in_group[d - 1],
        ))
    for copy in first_stage:
        copy.start()
    mine = part[pl.ds(member * share, share), :]
    for d, copy in enumerate(first_stage):
        copy.wait_recv()
        mine = mine + got1[d]

    def exchange(value, buffer, place, peers, send, recv):
        buffer[place] = value
        copies = [
            remote(buffer.at[place], buffer.at[place], send.at[d], recv.at[d], peer)
            for d, peer in enumerate(peers)
        ]
        for copy in copies:
            copy.start()
        for copy in copies:
            copy.wait_recv()
        started.extend(copies)
        value = buffer[0]
        for other in range(1, len(peers) + 1):
            value = value + buffer[other]
        return value

    if teams > 1:
        mine = exchange(mine, got2, team, in_teams, s4_sem, r4_sem)
    mine = exchange(mine, got3, me_z, in_z, s2_sem, r2_sem)

    home = pl.ds(member * share, share)
    out_ref[home, :] = mine
    last_stage = [
        remote(out_ref.at[home], out_ref.at[home], s3_sem.at[d], r3_sem.at[d], peer)
        for d, peer in enumerate(in_group)
    ]
    for copy in last_stage:
        copy.start()
    for copy in last_stage:
        copy.wait_recv()
    for copy in started + first_stage + last_stage:
        copy.wait_send()
    store.wait()


def orthonormal_rows(block, pivots):
    kept, snaps = block.shape
    inner = lax.dot_general(
        block, block, NT, precision=lax.Precision.HIGHEST, preferred_element_type=F32
    )
    groups = kept // 8
    left = [inner[8 * h : 8 * h + 8, :] for h in range(groups)]
    right = [block[8 * h : 8 * h + 8, :] for h in range(groups)]
    row_in = iota((8, snaps), 0)
    for k0 in range(0, kept, pivots):
        g, s0 = k0 // 8, k0 % 8
        ahead = range(pivots)
        cols = [
            [None] * g
            + [jnp.broadcast_to(left[h][:, k0 + n : k0 + n + 1], (8, snaps)) for h in range(g, groups)]
            for n in ahead
        ]
        own = [
            [jnp.broadcast_to(cols[n][g][s0 + j : s0 + j + 1, :], (8, snaps)) for n in ahead]
            for j in ahead
        ]
        lrow = [jnp.broadcast_to(left[g][s0 + j : s0 + j + 1, :], (8, kept)) for j in ahead]
        rrow = [jnp.broadcast_to(right[g][s0 + j : s0 + j + 1, :], (8, snaps)) for j in ahead]
        for j in ahead:
            pivot = own[j][j]
            guess = pl.reciprocal(pivot, approx=True)
            inverse = guess * (2.0 - pivot * guess)
            for n in range(j + 1, pivots):
                for m in range(n, pivots):
                    own[n][m] = own[n][m] - (own[j][n] * own[j][m]) * inverse
            for n in range(j + 1, pivots):
                times = own[j][n] * inverse
                lrow[n] = lrow[n] - times[:, :kept] * lrow[j]
                rrow[n] = rrow[n] - times * rrow[j]
                for h in range(g, groups):
                    cols[n][h] = cols[n][h] - times * cols[j][h]
            for h in range(g, groups):
                factor = cols[j][h] * inverse
                if h == g:
                    factor = jnp.where(row_in > s0 + j, factor, 0.0)
                left[h] = left[h] - factor[:, :kept] * lrow[j]
                right[h] = right[h] - factor * rrow[j]
            right[g] = jnp.where(row_in == s0 + j, rrow[j] * (inverse * jnp.sqrt(pivot)), right[g])
    return jnp.concatenate(right, axis=0)


def modes_kernel(dims, gram_ref, kept_ref, rank_ref, start_ref, modes_ref, basis_ref, flat_ref, spread, packed, sem, sems):
    snaps, planes, cx, cz, kept, nx, nz, group = dims
    fetch = pltpu.make_async_copy(kept_ref, flat_ref, sem)
    fetch.start()
    cells = float(planes * cx * nx * cz * nz)
    stride = planes * cx
    scale = jnp.where(rank_ref[...] < kept, 1.0, 0.25).astype(F32)
    down = jnp.transpose(jnp.broadcast_to(scale, (snaps, snaps)))
    weighted = down * (gram_ref[0:snaps, :] / cells) * scale

    def iterate(step, rows):
        moved = lax.dot_general(
            rows, weighted, NT, precision=lax.Precision.HIGHEST, preferred_element_type=F32
        )
        return orthonormal_rows(moved, 4)

    rows = lax.fori_loop(0, ITERS, iterate, start_ref[...])
    coef = (scale * rows).astype(BF16)
    anchor = jnp.sum(gram_ref[snaps : snaps + kept, :] * coef.astype(F32), axis=1, keepdims=True)
    orient = anchor / jnp.maximum(jnp.abs(anchor), 1.0)
    basis_ref[...] = rows * orient
    fetch.wait()
    for first in range(0, stride, 4):
        raw = orient * jnp.dot(
            coef, flat_ref[:, first * cz : (first + 4) * cz], preferred_element_type=F32
        )
        for n in range(4):
            spread[pl.ds(first + n, kept, stride=stride + 1), :] = raw[:, n * cz : (n + 1) * cz]

    def narrow(k, carry):
        block = spread[pl.ds(k * (stride + 1), stride), :]
        packed[pl.ds(pl.multiple_of(k * stride, 16), stride), :] = block.astype(BF16)
        return carry

    part = kept // 4
    writes = []
    for n in range(4):
        lax.fori_loop(n * part, (n + 1) * part, narrow, 0, unroll=True)
        here = pl.ds(n * part * stride, part * stride)
        writes.append(pltpu.make_async_copy(packed.at[here], modes_ref.at[here], sems.at[n]))
        writes[-1].start()
    for copy in writes:
        copy.wait()


def body(nx, nz, velocity, snapshot_rank, anchor_index, start_basis):
    _, snaps, planes, cx, cz = velocity.shape
    kept = start_basis.shape[1]
    total = snaps + kept
    group = max(g for g in (1, 2, 4, 8, 3, 6, 12, 24) if nx % g == 0 and total % (8 * g) == 0)
    dims = (snaps, planes, cx, cz, kept, nx, nz, group)
    rows = snaps * planes * cx
    share = total // group
    teams = nx // group
    vmem = pl.BlockSpec(memory_space=pltpu.VMEM)
    hbm = pl.BlockSpec(memory_space=pltpu.HBM)
    dma = lambda n: pltpu.SemaphoreType.DMA((max(n, 1),))
    flat, gram = pl.pallas_call(
        functools.partial(gram_kernel, dims),
        out_shape=(
            jax.ShapeDtypeStruct((snaps, planes * cx * cz), BF16),
            jax.ShapeDtypeStruct((total, snaps), F32),
        ),
        in_specs=[hbm] * 2,
        out_specs=(hbm, vmem),
        scratch_shapes=[
            pltpu.VMEM((snaps, planes * cx * cz), BF16),
            pltpu.VMEM((rows, cz), BF16),
            pltpu.VMEM((rows, cz), BF16),
            pltpu.VMEM((1, kept), jnp.int32),
            pltpu.VMEM((rows + snaps, cz), F32),
            pltpu.VMEM((rows + snaps, cz), F32),
            pltpu.VMEM((2, planes * REACH, snaps, cz), BF16),
            pltpu.VMEM((2, planes * REACH, snaps, cz), BF16),
            pltpu.VMEM((2, 16, rows // 4), BF16),
            pltpu.VMEM((2, 16, rows // 4), BF16),
            pltpu.VMEM((total, snaps), F32),
            pltpu.VMEM((max(group - 1, 1), share, snaps), F32),
            pltpu.VMEM((teams, share, snaps), F32),
            pltpu.VMEM((nz, share, snaps), F32),
            dma(2), dma(2), dma(2), dma(2),
            dma(group - 1), dma(group - 1),
            dma(nz - 1), dma(nz - 1),
            dma(group - 1), dma(group - 1),
            dma(teams - 1), dma(teams - 1), dma(10),
        ],
        compiler_params=pltpu.CompilerParams(
            collective_id=0, has_side_effects=True, vmem_limit_bytes=58 * 1024 * 1024
        ),
        name="vorticity_gram",
    )(velocity.reshape(2, rows, cz), anchor_index.reshape(1, kept))
    modes, basis = pl.pallas_call(
        functools.partial(modes_kernel, dims),
        out_shape=(
            jax.ShapeDtypeStruct((kept * planes * cx, cz), BF16),
            jax.ShapeDtypeStruct((kept, snaps), F32),
        ),
        in_specs=[vmem, hbm, vmem, vmem],
        out_specs=(hbm, vmem),
        scratch_shapes=[
            pltpu.VMEM((snaps, planes * cx * cz), BF16),
            pltpu.VMEM((kept * (planes * cx + 1), cz), F32),
            pltpu.VMEM((kept * planes * cx, cz), BF16),
            pltpu.SemaphoreType.DMA,
            dma(4),
        ],
        compiler_params=pltpu.CompilerParams(vmem_limit_bytes=58 * 1024 * 1024),
        name="subspace_modes",
    )(gram, flat, snapshot_rank.reshape(1, snaps), start_basis.T)
    return modes.reshape(kept, planes, cx, cz), basis.T


def solution(mesh):
    return jax.shard_map(
        functools.partial(body, mesh.shape["gx"], mesh.shape["gz"]),
        mesh=mesh,
        in_specs=(P(None, None, None, "gx", "gz"), P(), P(), P()),
        out_specs=(P(None, None, "gx", "gz"), P()),
        check_vma=False,
    )
```

```python
import functools
import jax
import jax.numpy as jnp
from jax import lax
from jax.experimental import pallas as pl
from jax.experimental.pallas import tpu as pltpu
from jax.sharding import PartitionSpec as P

ITERS = 3
REACH = 3
MESH = pl.DeviceIdType.MESH
NT = (((1,), (1,)), ((), ()))
F32 = jnp.float32
BF16 = jnp.bfloat16


def iota(shape, dim):
    return lax.broadcasted_iota(jnp.int32, shape, dim)


def stencil_weight(offset):
    size = jnp.abs(offset)
    value = jnp.where(size == 1, 45, jnp.where(size == 2, -9, jnp.where(size == 3, 1, 0)))
    return jnp.where(offset < 0, -value, value).astype(F32).astype(BF16)


def gram_kernel(
    dims, vel_ref, anchor_ref, kept_ref, out_ref,
    flat_ref, spans, streams, spots, wide, uterm, sendx, recvx, sendz, recvz, part, got1, got2, got3,
    sx_sem, rx_sem, sz_sem, rz_sem, s1_sem, r1_sem, s2_sem, r2_sem, s3_sem, r3_sem, s4_sem, r4_sem, load_sem,
):
    snaps, planes, cx, cz, kept, nx, nz, group = dims
    rows = snaps * planes * cx
    stride = planes * cx
    pitch = stride + 1
    me_x = lax.axis_index("gx")
    me_z = lax.axis_index("gz")
    member = lax.rem(me_x, group)
    base = me_x - member
    teams = nx // group
    team = me_x // group
    share = part.shape[0] // group
    xnext, xprev = lax.rem(me_x + 1, nx), lax.rem(me_x + nx - 1, nx)
    znext, zprev = lax.rem(me_z + 1, nz), lax.rem(me_z + nz - 1, nz)

    in_group = [(base + lax.rem(member + d, group), me_z) for d in range(1, group)]
    in_teams = [(lax.rem(team + d, teams) * group + member, me_z) for d in range(1, teams)]
    in_z = [(me_x, lax.rem(me_z + d, nz)) for d in range(1, nz)]
    greet = in_group + in_teams + in_z
    if teams > 1:
        greet = greet + [(xnext, me_z), (xprev, me_z)]

    quarter = rows // 4
    loads = []
    for half, kept_in in ((0, spans), (1, streams)):
        for c in range(4):
            here = pl.ds(c * quarter, quarter)
            loads.append(pltpu.make_async_copy(
                vel_ref.at[half, here], kept_in.at[here], load_sem.at[half * 4 + c]
            ))
    loads.append(pltpu.make_async_copy(anchor_ref, spots, load_sem.at[8]))
    barrier = pltpu.get_barrier_semaphore()
    for peer in greet:
        pl.semaphore_signal(barrier, inc=1, device_id=peer, device_id_type=MESH)
    for copy in loads[:4] + loads[8:]:
        copy.start()

    def remote(src, dst, send, recv, peer):
        return pltpu.make_async_remote_copy(
            src_ref=src, dst_ref=dst, send_sem=send, recv_sem=recv,
            device_id=peer, device_id_type=MESH,
        )

    edge = iota((32, cz), 0)
    lane = iota((32, cz), 1)
    packed = jnp.zeros((32, quarter), F32)
    for c in range(4):
        r = edge % 16 - 4 * c
        wanted = jnp.where(edge < 16, cz - REACH + r, r)
        pick = jnp.where((r >= 0) & (r < REACH) & (lane == wanted), 1.0, 0.0).astype(BF16)
        loads[c].wait()
        loads[4 + c].start()
        packed = packed + lax.dot_general(
            pick, spans[c * quarter : (c + 1) * quarter, :], NT, preferred_element_type=F32
        )
    sendz[...] = packed.astype(BF16).reshape(2, 16, quarter)
    pl.semaphore_wait(barrier, len(greet))
    halos = [
        remote(sendz.at[0], recvz.at[0], sz_sem.at[0], rz_sem.at[0], (me_x, znext)),
        remote(sendz.at[1], recvz.at[1], sz_sem.at[1], rz_sem.at[1], (me_x, zprev)),
        remote(sendx.at[0], recvx.at[0], sx_sem.at[0], rx_sem.at[0], (xnext, me_z)),
        remote(sendx.at[1], recvx.at[1], sx_sem.at[1], rx_sem.at[1], (xprev, me_z)),
    ]
    halos[0].start()
    halos[1].start()

    some = snaps // 4
    for c in range(4):
        loads[4 + c].wait()

        def widen(m, carry, first=c * some):
            at = pl.multiple_of((first + m) * stride, 16)
            wide[pl.ds((first + m) * pitch, stride), :] = streams[pl.ds(at, stride), :].astype(F32)
            return carry

        lax.fori_loop(0, some, widen, 0, unroll=8)
        for p in range(planes):
            for r in range(REACH):
                low = c * some * pitch + p * cx + r
                block = wide[pl.ds(low + cx - REACH, some, stride=pitch), :]
                sendx[0, p * REACH + r, c * some : (c + 1) * some, :] = block.astype(BF16)
                block = wide[pl.ds(low, some, stride=pitch), :]
                sendx[1, p * REACH + r, c * some : (c + 1) * some, :] = block.astype(BF16)
    halos[2].start()
    halos[3].start()

    loads[8].wait()
    index = spots[...]
    total_x, total_z = cx * nx, cz * nz
    plane_of = index // (total_x * total_z)
    remain = index % (total_x * total_z)
    local_x = remain // total_z - me_x * cx
    local_z = remain % total_z - me_z * cz
    owned = (local_x >= 0) & (local_x < cx) & (local_z >= 0) & (local_z < cz)
    position = jnp.where(owned, (plane_of * cx + local_x) * cz + local_z, -1).astype(F32)
    column = jnp.transpose(jnp.broadcast_to(position, (kept, kept)))[:, 0:1]

    band = stencil_weight(iota((cz, cz), 1) - iota((cz, cz), 0))
    halos[0].wait_recv()
    halos[1].wait_recv()
    sides = jnp.transpose(recvz[...].reshape(32, quarter).astype(F32)).astype(BF16)

    def spanwise(c, carry):
        r = edge % 16 - 4 * c
        source = jnp.where(edge < 16, r - REACH, cz + r)
        valid = (r >= 0) & (r < REACH)
        spread = stencil_weight(jnp.where(valid, lane - source, 0))
        here = pl.ds(pl.multiple_of(c * quarter, 16), quarter)
        value = jnp.dot(
            spans[here, :], band, preferred_element_type=F32
        ) + jnp.dot(sides, spread, preferred_element_type=F32)
        for m in range(some):
            at = pl.ds((c * some + m) * pitch, stride)
            uterm[at, :] = value[m * stride : (m + 1) * stride, :]
        return carry

    lax.fori_loop(0, 4, spanwise, 0)

    def snapshots(*spans_x):
        def some_rows(step, carry):
            first = pl.multiple_of(step * 16, 16)
            for p in range(planes):
                layers = {}
                needed = {x + d for begin, end in spans_x for x in range(begin, end) for d in range(-REACH, REACH + 1)}
                for x in sorted(needed):
                    if x < 0:
                        block = recvx[0, p * REACH + x + REACH, pl.ds(first, 16), :].astype(F32)
                    elif x >= cx:
                        block = recvx[1, p * REACH + x - cx, pl.ds(first, 16), :].astype(F32)
                    else:
                        block = wide[pl.ds(first * pitch + p * cx + x, 16, stride=pitch), :]
                    layers[x] = block
                for x in [x for begin, end in spans_x for x in range(begin, end)]:
                    value = 45.0 * (layers[x + 1] - layers[x - 1])
                    value = value - 9.0 * (layers[x + 2] - layers[x - 2])
                    value = value + (layers[x + 3] - layers[x - 3])
                    value = value + uterm[pl.ds(first * pitch + p * cx + x, 16, stride=pitch), :]
                    cell = (p * cx + x) * cz
                    flat_ref[pl.ds(first, 16), cell : cell + cz] = (value * (1.0 / 60.0)).astype(BF16)
            return carry

        lax.fori_loop(0, snaps // 16, some_rows, 0)

    def products(begin, end):
        total = jnp.zeros((snaps + kept, snaps), F32)
        for p in range(planes):
            cell, width = (p * cx + begin) * cz, (end - begin) * cz
            block = flat_ref[:, cell : cell + width]
            cell_in = iota((kept, width), 1).astype(F32) + float(cell)
            mark = jnp.where(cell_in == column, 1.0, 0.0).astype(BF16)
            both = jnp.concatenate([block, mark], axis=0)
            total = total + lax.dot_general(both, block, NT, preferred_element_type=F32)
        return total

    snapshots((REACH, cx - REACH))
    part[...] = products(REACH, cx - REACH)
    halos[2].wait_recv()
    halos[3].wait_recv()
    snapshots((0, REACH), (cx - REACH, cx))
    store = pltpu.make_async_copy(flat_ref, kept_ref, load_sem.at[9])
    store.start()
    part[...] += products(0, REACH) + products(cx - REACH, cx)

    started = list(halos)
    first_stage = []
    for d in range(1, group):
        target = lax.rem(member + d, group)
        first_stage.append(remote(
            part.at[pl.ds(target * share, share)], got1.at[d - 1],
            s1_sem.at[d - 1], r1_sem.at[d - 1], in_group[d - 1],
        ))
    for copy in first_stage:
        copy.start()
    mine = part[pl.ds(member * share, share), :]
    for d, copy in enumerate(first_stage):
        copy.wait_recv()
        mine = mine + got1[d]

    def exchange(value, buffer, place, peers, send, recv):
        buffer[place] = value
        copies = [
            remote(buffer.at[place], buffer.at[place], send.at[d], recv.at[d], peer)
            for d, peer in enumerate(peers)
        ]
        for copy in copies:
            copy.start()
        for copy in copies:
            copy.wait_recv()
        started.extend(copies)
        value = buffer[0]
        for other in range(1, len(peers) + 1):
            value = value + buffer[other]
        return value

    if teams > 1:
        mine = exchange(mine, got2, team, in_teams, s4_sem, r4_sem)
    mine = exchange(mine, got3, me_z, in_z, s2_sem, r2_sem)

    home = pl.ds(member * share, share)
    out_ref[home, :] = mine
    last_stage = [
        remote(out_ref.at[home], out_ref.at[home], s3_sem.at[d], r3_sem.at[d], peer)
        for d, peer in enumerate(in_group)
    ]
    for copy in last_stage:
        copy.start()
    for copy in last_stage:
        copy.wait_recv()
    for copy in started + first_stage + last_stage:
        copy.wait_send()
    store.wait()


def orthonormal_rows(block, pivots):
    kept, snaps = block.shape
    inner = lax.dot_general(
        block, block, NT, precision=lax.Precision.HIGHEST, preferred_element_type=F32
    )
    groups = kept // 8
    left = [inner[8 * h : 8 * h + 8, :] for h in range(groups)]
    right = [block[8 * h : 8 * h + 8, :] for h in range(groups)]
    row_in = iota((8, snaps), 0)
    for k0 in range(0, kept, pivots):
        g, s0 = k0 // 8, k0 % 8
        ahead = range(pivots)
        cols = [
            [None] * g
            + [jnp.broadcast_to(left[h][:, k0 + n : k0 + n + 1], (8, snaps)) for h in range(g, groups)]
            for n in ahead
        ]
        own = [
            [jnp.broadcast_to(cols[n][g][s0 + j : s0 + j + 1, :], (8, snaps)) for n in ahead]
            for j in ahead
        ]
        lrow = [jnp.broadcast_to(left[g][s0 + j : s0 + j + 1, :], (8, kept)) for j in ahead]
        rrow = [jnp.broadcast_to(right[g][s0 + j : s0 + j + 1, :], (8, snaps)) for j in ahead]
        for j in ahead:
            pivot = own[j][j]
            inverse = 1.0 / pivot
            for n in range(j + 1, pivots):
                for m in range(n, pivots):
                    own[n][m] = own[n][m] - (own[j][n] * own[j][m]) * inverse
            for n in range(j + 1, pivots):
                times = own[j][n] * inverse
                lrow[n] = lrow[n] - times[:, :kept] * lrow[j]
                rrow[n] = rrow[n] - times * rrow[j]
                for h in range(g, groups):
                    cols[n][h] = cols[n][h] - times * cols[j][h]
            for h in range(g, groups):
                factor = cols[j][h] * inverse
                if h == g:
                    factor = jnp.where(row_in > s0 + j, factor, 0.0)
                left[h] = left[h] - factor[:, :kept] * lrow[j]
                right[h] = right[h] - factor * rrow[j]
            right[g] = jnp.where(row_in == s0 + j, rrow[j] * (inverse * jnp.sqrt(pivot)), right[g])
    return jnp.concatenate(right, axis=0)


def modes_kernel(dims, gram_ref, kept_ref, rank_ref, start_ref, modes_ref, basis_ref, flat_ref, spread, sem):
    snaps, planes, cx, cz, kept, nx, nz, group = dims
    fetch = pltpu.make_async_copy(kept_ref, flat_ref, sem)
    fetch.start()
    cells = float(planes * cx * nx * cz * nz)
    stride = planes * cx
    scale = jnp.where(rank_ref[...] < kept, 1.0, 0.25).astype(F32)
    down = jnp.transpose(jnp.broadcast_to(scale, (snaps, snaps)))
    weighted = down * (gram_ref[0:snaps, :] / cells) * scale

    def iterate(step, rows):
        moved = lax.dot_general(
            rows, weighted, NT, precision=lax.Precision.HIGHEST, preferred_element_type=F32
        )
        return orthonormal_rows(moved, 8)

    rows = lax.fori_loop(0, ITERS, iterate, start_ref[...])
    coef = (scale * rows).astype(BF16)
    anchor = jnp.sum(gram_ref[snaps : snaps + kept, :] * coef.astype(F32), axis=1, keepdims=True)
    orient = anchor / jnp.maximum(jnp.abs(anchor), 1.0)
    basis_ref[...] = rows * orient
    fetch.wait()
    for first in range(0, stride, 4):
        raw = orient * jnp.dot(
            coef, flat_ref[:, first * cz : (first + 4) * cz], preferred_element_type=F32
        )
        for n in range(4):
            spread[pl.ds(first + n, kept, stride=stride + 1), :] = raw[:, n * cz : (n + 1) * cz]

    def narrow(k, carry):
        block = spread[pl.ds(k * (stride + 1), stride), :]
        modes_ref[pl.ds(pl.multiple_of(k * stride, 16), stride), :] = block.astype(BF16)
        return carry

    lax.fori_loop(0, kept, narrow, 0, unroll=8)


def body(nx, nz, velocity, snapshot_rank, anchor_index, start_basis):
    _, snaps, planes, cx, cz = velocity.shape
    kept = start_basis.shape[1]
    total = snaps + kept
    group = max(g for g in (1, 2, 4, 8, 3, 6, 12, 24) if nx % g == 0 and total % (8 * g) == 0)
    dims = (snaps, planes, cx, cz, kept, nx, nz, group)
    rows = snaps * planes * cx
    share = total // group
    teams = nx // group
    vmem = pl.BlockSpec(memory_space=pltpu.VMEM)
    hbm = pl.BlockSpec(memory_space=pltpu.HBM)
    dma = lambda n: pltpu.SemaphoreType.DMA((max(n, 1),))
    flat, gram = pl.pallas_call(
        functools.partial(gram_kernel, dims),
        out_shape=(
            jax.ShapeDtypeStruct((snaps, planes * cx * cz), BF16),
            jax.ShapeDtypeStruct((total, snaps), F32),
        ),
        in_specs=[hbm] * 2,
        out_specs=(hbm, vmem),
        scratch_shapes=[
            pltpu.VMEM((snaps, planes * cx * cz), BF16),
            pltpu.VMEM((rows, cz), BF16),
            pltpu.VMEM((rows, cz), BF16),
            pltpu.VMEM((1, kept), jnp.int32),
            pltpu.VMEM((rows + snaps, cz), F32),
            pltpu.VMEM((rows + snaps, cz), F32),
            pltpu.VMEM((2, planes * REACH, snaps, cz), BF16),
            pltpu.VMEM((2, planes * REACH, snaps, cz), BF16),
            pltpu.VMEM((2, 16, rows // 4), BF16),
            pltpu.VMEM((2, 16, rows // 4), BF16),
            pltpu.VMEM((total, snaps), F32),
            pltpu.VMEM((max(group - 1, 1), share, snaps), F32),
            pltpu.VMEM((teams, share, snaps), F32),
            pltpu.VMEM((nz, share, snaps), F32),
            dma(2), dma(2), dma(2), dma(2),
            dma(group - 1), dma(group - 1),
            dma(nz - 1), dma(nz - 1),
            dma(group - 1), dma(group - 1),
            dma(teams - 1), dma(teams - 1), dma(10),
        ],
        compiler_params=pltpu.CompilerParams(
            collective_id=0, has_side_effects=True, vmem_limit_bytes=58 * 1024 * 1024
        ),
        name="vorticity_gram",
    )(velocity.reshape(2, rows, cz), anchor_index.reshape(1, kept))
    modes, basis = pl.pallas_call(
        functools.partial(modes_kernel, dims),
        out_shape=(
            jax.ShapeDtypeStruct((kept * planes * cx, cz), BF16),
            jax.ShapeDtypeStruct((kept, snaps), F32),
        ),
        in_specs=[vmem, hbm, vmem, vmem],
        out_specs=(vmem, vmem),
        scratch_shapes=[
            pltpu.VMEM((snaps, planes * cx * cz), BF16),
            pltpu.VMEM((kept * (planes * cx + 1), cz), F32),
            pltpu.SemaphoreType.DMA,
        ],
        compiler_params=pltpu.CompilerParams(vmem_limit_bytes=58 * 1024 * 1024),
        name="subspace_modes",
    )(gram, flat, snapshot_rank.reshape(1, snaps), start_basis.T)
    return modes.reshape(kept, planes, cx, cz), basis.T


def solution(mesh):
    return jax.shard_map(
        functools.partial(body, mesh.shape["gx"], mesh.shape["gz"]),
        mesh=mesh,
        in_specs=(P(None, None, None, "gx", "gz"), P(), P(), P()),
        out_specs=(P(None, None, "gx", "gz"), P()),
        check_vma=False,
    )
```

```python
import functools
import jax
import jax.numpy as jnp
from jax import lax
from jax.experimental import pallas as pl
from jax.experimental.pallas import tpu as pltpu
from jax.sharding import PartitionSpec as P

ITERS = 3
REACH = 3
MESH = pl.DeviceIdType.MESH
NT = (((1,), (1,)), ((), ()))
F32 = jnp.float32
BF16 = jnp.bfloat16


def iota(shape, dim):
    return lax.broadcasted_iota(jnp.int32, shape, dim)


def stencil_weight(offset):
    size = jnp.abs(offset)
    value = jnp.where(size == 1, 45, jnp.where(size == 2, -9, jnp.where(size == 3, 1, 0)))
    return jnp.where(offset < 0, -value, value).astype(F32).astype(BF16)


def gram_kernel(
    dims, vel_ref, anchor_ref, kept_ref, out_ref,
    flat_ref, spans, streams, spots, wide, uterm, sendx, recvx, sendz, recvz, part, got1, got2, got3,
    sx_sem, rx_sem, sz_sem, rz_sem, s1_sem, r1_sem, s2_sem, r2_sem, s3_sem, r3_sem, s4_sem, r4_sem, load_sem,
):
    snaps, planes, cx, cz, kept, nx, nz, group = dims
    rows = snaps * planes * cx
    stride = planes * cx
    pitch = stride + 1
    me_x = lax.axis_index("gx")
    me_z = lax.axis_index("gz")
    member = lax.rem(me_x, group)
    base = me_x - member
    teams = nx // group
    team = me_x // group
    share = part.shape[0] // group
    xnext, xprev = lax.rem(me_x + 1, nx), lax.rem(me_x + nx - 1, nx)
    znext, zprev = lax.rem(me_z + 1, nz), lax.rem(me_z + nz - 1, nz)

    in_group = [(base + lax.rem(member + d, group), me_z) for d in range(1, group)]
    in_teams = [(lax.rem(team + d, teams) * group + member, me_z) for d in range(1, teams)]
    in_z = [(me_x, lax.rem(me_z + d, nz)) for d in range(1, nz)]
    greet = in_group + in_teams + in_z
    if teams > 1:
        greet = greet + [(xnext, me_z), (xprev, me_z)]

    quarter = rows // 4
    loads = []
    for half, kept_in in ((0, spans), (1, streams)):
        for c in range(4):
            here = pl.ds(c * quarter, quarter)
            loads.append(pltpu.make_async_copy(
                vel_ref.at[half, here], kept_in.at[here], load_sem.at[half * 4 + c]
            ))
    loads.append(pltpu.make_async_copy(anchor_ref, spots, load_sem.at[8]))
    barrier = pltpu.get_barrier_semaphore()
    for peer in greet:
        pl.semaphore_signal(barrier, inc=1, device_id=peer, device_id_type=MESH)
    for copy in loads[:4] + loads[8:]:
        copy.start()

    def remote(src, dst, send, recv, peer):
        return pltpu.make_async_remote_copy(
            src_ref=src, dst_ref=dst, send_sem=send, recv_sem=recv,
            device_id=peer, device_id_type=MESH,
        )

    edge = iota((32, cz), 0)
    lane = iota((32, cz), 1)
    packed = jnp.zeros((32, quarter), F32)
    for c in range(4):
        r = edge % 16 - 4 * c
        wanted = jnp.where(edge < 16, cz - REACH + r, r)
        pick = jnp.where((r >= 0) & (r < REACH) & (lane == wanted), 1.0, 0.0).astype(BF16)
        loads[c].wait()
        loads[4 + c].start()
        packed = packed + lax.dot_general(
            pick, spans[c * quarter : (c + 1) * quarter, :], NT, preferred_element_type=F32
        )
    sendz[...] = packed.astype(BF16).reshape(2, 16, quarter)
    pl.semaphore_wait(barrier, len(greet))
    halos = [
        remote(sendz.at[0], recvz.at[0], sz_sem.at[0], rz_sem.at[0], (me_x, znext)),
        remote(sendz.at[1], recvz.at[1], sz_sem.at[1], rz_sem.at[1], (me_x, zprev)),
        remote(sendx.at[0], recvx.at[0], sx_sem.at[0], rx_sem.at[0], (xnext, me_z)),
        remote(sendx.at[1], recvx.at[1], sx_sem.at[1], rx_sem.at[1], (xprev, me_z)),
    ]
    halos[0].start()
    halos[1].start()

    some = snaps // 4
    for c in range(4):
        loads[4 + c].wait()

        def widen(m, carry, first=c * some):
            at = pl.multiple_of((first + m) * stride, 16)
            wide[pl.ds((first + m) * pitch, stride), :] = streams[pl.ds(at, stride), :].astype(F32)
            return carry

        lax.fori_loop(0, some, widen, 0, unroll=8)
        for p in range(planes):
            for r in range(REACH):
                low = c * some * pitch + p * cx + r
                block = wide[pl.ds(low + cx - REACH, some, stride=pitch), :]
                sendx[0, p * REACH + r, c * some : (c + 1) * some, :] = block.astype(BF16)
                block = wide[pl.ds(low, some, stride=pitch), :]
                sendx[1, p * REACH + r, c * some : (c + 1) * some, :] = block.astype(BF16)
    halos[2].start()
    halos[3].start()

    loads[8].wait()
    index = spots[...]
    total_x, total_z = cx * nx, cz * nz
    plane_of = index // (total_x * total_z)
    remain = index % (total_x * total_z)
    local_x = remain // total_z - me_x * cx
    local_z = remain % total_z - me_z * cz
    owned = (local_x >= 0) & (local_x < cx) & (local_z >= 0) & (local_z < cz)
    position = jnp.where(owned, (plane_of * cx + local_x) * cz + local_z, -1).astype(F32)
    column = jnp.transpose(jnp.broadcast_to(position, (kept, kept)))[:, 0:1]

    band = stencil_weight(iota((cz, cz), 1) - iota((cz, cz), 0))
    halos[0].wait_recv()
    halos[1].wait_recv()
    sides = jnp.transpose(recvz[...].reshape(32, quarter).astype(F32)).astype(BF16)

    def spanwise(c, carry):
        r = edge % 16 - 4 * c
        source = jnp.where(edge < 16, r - REACH, cz + r)
        valid = (r >= 0) & (r < REACH)
        spread = stencil_weight(jnp.where(valid, lane - source, 0))
        here = pl.ds(pl.multiple_of(c * quarter, 16), quarter)
        value = jnp.dot(
            spans[here, :], band, preferred_element_type=F32
        ) + jnp.dot(sides, spread, preferred_element_type=F32)
        for m in range(some):
            at = pl.ds((c * some + m) * pitch, stride)
            uterm[at, :] = value[m * stride : (m + 1) * stride, :]
        return carry

    lax.fori_loop(0, 4, spanwise, 0)

    def snapshots(*spans_x):
        def some_rows(step, carry):
            first = pl.multiple_of(step * 16, 16)
            for p in range(planes):
                layers = {}
                needed = {x + d for begin, end in spans_x for x in range(begin, end) for d in range(-REACH, REACH + 1)}
                for x in sorted(needed):
                    if x < 0:
                        block = recvx[0, p * REACH + x + REACH, pl.ds(first, 16), :].astype(F32)
                    elif x >= cx:
                        block = recvx[1, p * REACH + x - cx, pl.ds(first, 16), :].astype(F32)
                    else:
                        block = wide[pl.ds(first * pitch + p * cx + x, 16, stride=pitch), :]
                    layers[x] = block
                for x in [x for begin, end in spans_x for x in range(begin, end)]:
                    value = 45.0 * (layers[x + 1] - layers[x - 1])
                    value = value - 9.0 * (layers[x + 2] - layers[x - 2])
                    value = value + (layers[x + 3] - layers[x - 3])
                    value = value + uterm[pl.ds(first * pitch + p * cx + x, 16, stride=pitch), :]
                    cell = (p * cx + x) * cz
                    flat_ref[pl.ds(first, 16), cell : cell + cz] = (value * (1.0 / 60.0)).astype(BF16)
            return carry

        lax.fori_loop(0, snaps // 16, some_rows, 0)

    def products(begin, end):
        total = jnp.zeros((snaps + kept, snaps), F32)
        for p in range(planes):
            cell, width = (p * cx + begin) * cz, (end - begin) * cz
            block = flat_ref[:, cell : cell + width]
            cell_in = iota((kept, width), 1).astype(F32) + float(cell)
            mark = jnp.where(cell_in == column, 1.0, 0.0).astype(BF16)
            both = jnp.concatenate([block, mark], axis=0)
            total = total + lax.dot_general(both, block, NT, preferred_element_type=F32)
        return total

    snapshots((REACH, cx - REACH))
    part[...] = products(REACH, cx - REACH)
    halos[2].wait_recv()
    halos[3].wait_recv()
    snapshots((0, REACH), (cx - REACH, cx))
    store = pltpu.make_async_copy(flat_ref, kept_ref, load_sem.at[9])
    store.start()
    part[...] += products(0, REACH) + products(cx - REACH, cx)

    started = list(halos)
    first_stage = []
    for d in range(1, group):
        target = lax.rem(member + d, group)
        first_stage.append(remote(
            part.at[pl.ds(target * share, share)], got1.at[d - 1],
            s1_sem.at[d - 1], r1_sem.at[d - 1], in_group[d - 1],
        ))
    for copy in first_stage:
        copy.start()
    mine = part[pl.ds(member * share, share), :]
    for d, copy in enumerate(first_stage):
        copy.wait_recv()
        mine = mine + got1[d]

    def exchange(value, buffer, place, peers, send, recv):
        buffer[place] = value
        copies = [
            remote(buffer.at[place], buffer.at[place], send.at[d], recv.at[d], peer)
            for d, peer in enumerate(peers)
        ]
        for copy in copies:
            copy.start()
        for copy in copies:
            copy.wait_recv()
        started.extend(copies)
        value = buffer[0]
        for other in range(1, len(peers) + 1):
            value = value + buffer[other]
        return value

    if teams > 1:
        mine = exchange(mine, got2, team, in_teams, s4_sem, r4_sem)
    mine = exchange(mine, got3, me_z, in_z, s2_sem, r2_sem)

    home = pl.ds(member * share, share)
    out_ref[home, :] = mine
    last_stage = [
        remote(out_ref.at[home], out_ref.at[home], s3_sem.at[d], r3_sem.at[d], peer)
        for d, peer in enumerate(in_group)
    ]
    for copy in last_stage:
        copy.start()
    for copy in last_stage:
        copy.wait_recv()
    for copy in started + first_stage + last_stage:
        copy.wait_send()
    store.wait()


def orthonormal_rows(block):
    kept, snaps = block.shape
    inner = lax.dot_general(
        block, block, NT, precision=lax.Precision.HIGHEST, preferred_element_type=F32
    )
    groups = kept // 8
    left = [inner[8 * h : 8 * h + 8, :] for h in range(groups)]
    right = [block[8 * h : 8 * h + 8, :] for h in range(groups)]
    row_in = iota((8, snaps), 0)
    eight = range(8)
    for g in range(groups):
        below = range(g + 1, groups)
        cols = [
            {h: jnp.broadcast_to(left[h][:, 8 * g + n : 8 * g + n + 1], (8, snaps)) for h in range(g, groups)}
            for n in eight
        ]
        own = [
            [jnp.broadcast_to(cols[n][g][j : j + 1, :], (8, snaps)) for n in eight] for j in eight
        ]
        lrow = [jnp.broadcast_to(left[g][j : j + 1, :], (8, kept)) for j in eight]
        rrow = [jnp.broadcast_to(right[g][j : j + 1, :], (8, snaps)) for j in eight]

        def clear(j, n, times):
            lrow[n] = lrow[n] - times[:, :kept] * lrow[j]
            rrow[n] = rrow[n] - times * rrow[j]
            for h in below:
                cols[n][h] = cols[n][h] - times * cols[j][h]

        for j in range(0, 8, 2):
            first, cross = own[j][j], own[j][j + 1]
            det = first * own[j + 1][j + 1] - cross * cross
            one = 1.0 / first
            two = first * (1.0 / det)
            ratio = cross * one
            for n in range(j + 2, 8):
                own[j + 1][n] = own[j + 1][n] - ratio * own[j][n]
            for n in range(j + 2, 8):
                for m in range(n, 8):
                    own[n][m] = own[n][m] - (own[j][n] * own[j][m]) * one
                    own[n][m] = own[n][m] - (own[j + 1][n] * own[j + 1][m]) * two
            clear(j, j + 1, ratio)
            for n in range(j + 2, 8):
                clear(j, n, own[j][n] * one)
                clear(j + 1, n, own[j + 1][n] * two)
            for i, inverse in ((j, one), (j + 1, two)):
                for h in below:
                    factor = cols[i][h] * inverse
                    left[h] = left[h] - factor[:, :kept] * lrow[i]
                    right[h] = right[h] - factor * rrow[i]
                done = rrow[i] * jnp.sqrt(inverse)
                right[g] = done if i == 0 else jnp.where(row_in == i, done, right[g])
    return jnp.concatenate(right, axis=0)


def modes_kernel(dims, gram_ref, kept_ref, rank_ref, start_ref, modes_ref, basis_ref, flat_ref, spread, sem):
    snaps, planes, cx, cz, kept, nx, nz, group = dims
    fetch = pltpu.make_async_copy(kept_ref, flat_ref, sem)
    fetch.start()
    cells = float(planes * cx * nx * cz * nz)
    stride = planes * cx
    scale = jnp.where(rank_ref[...] < kept, 1.0, 0.25).astype(F32)
    down = jnp.transpose(jnp.broadcast_to(scale, (snaps, snaps)))
    weighted = down * (gram_ref[0:snaps, :] / cells) * scale
    diagonal = iota((snaps, snaps), 0) == iota((snaps, snaps), 1)
    weighted = weighted / jnp.sum(jnp.where(diagonal, weighted, 0.0))
    start = start_ref[...]
    start = start / jnp.max(jnp.abs(start), axis=1, keepdims=True)

    def iterate(step, rows):
        moved = lax.dot_general(
            rows, weighted, NT, precision=lax.Precision.HIGHEST, preferred_element_type=F32
        )
        return orthonormal_rows(moved)

    rows = lax.fori_loop(0, ITERS, iterate, start)
    coef = (scale * rows).astype(BF16)
    anchor = jnp.sum(gram_ref[snaps : snaps + kept, :] * coef.astype(F32), axis=1, keepdims=True)
    orient = anchor / jnp.maximum(jnp.abs(anchor), 1.0)
    basis_ref[...] = rows * orient
    fetch.wait()
    for first in range(0, stride, 4):
        raw = orient * jnp.dot(
            coef, flat_ref[:, first * cz : (first + 4) * cz], preferred_element_type=F32
        )
        for n in range(4):
            spread[pl.ds(first + n, kept, stride=stride + 1), :] = raw[:, n * cz : (n + 1) * cz]

    def narrow(k, carry):
        block = spread[pl.ds(k * (stride + 1), stride), :]
        modes_ref[pl.ds(pl.multiple_of(k * stride, 16), stride), :] = block.astype(BF16)
        return carry

    lax.fori_loop(0, kept, narrow, 0, unroll=8)


def body(nx, nz, velocity, snapshot_rank, anchor_index, start_basis):
    _, snaps, planes, cx, cz = velocity.shape
    kept = start_basis.shape[1]
    total = snaps + kept
    group = max(g for g in (1, 2, 4, 8, 3, 6, 12, 24) if nx % g == 0 and total % (8 * g) == 0)
    dims = (snaps, planes, cx, cz, kept, nx, nz, group)
    rows = snaps * planes * cx
    share = total // group
    teams = nx // group
    vmem = pl.BlockSpec(memory_space=pltpu.VMEM)
    hbm = pl.BlockSpec(memory_space=pltpu.HBM)
    dma = lambda n: pltpu.SemaphoreType.DMA((max(n, 1),))
    flat, gram = pl.pallas_call(
        functools.partial(gram_kernel, dims),
        out_shape=(
            jax.ShapeDtypeStruct((snaps, planes * cx * cz), BF16),
            jax.ShapeDtypeStruct((total, snaps), F32),
        ),
        in_specs=[hbm] * 2,
        out_specs=(hbm, vmem),
        scratch_shapes=[
            pltpu.VMEM((snaps, planes * cx * cz), BF16),
            pltpu.VMEM((rows, cz), BF16),
            pltpu.VMEM((rows, cz), BF16),
            pltpu.VMEM((1, kept), jnp.int32),
            pltpu.VMEM((rows + snaps, cz), F32),
            pltpu.VMEM((rows + snaps, cz), F32),
            pltpu.VMEM((2, planes * REACH, snaps, cz), BF16),
            pltpu.VMEM((2, planes * REACH, snaps, cz), BF16),
            pltpu.VMEM((2, 16, rows // 4), BF16),
            pltpu.VMEM((2, 16, rows // 4), BF16),
            pltpu.VMEM((total, snaps), F32),
            pltpu.VMEM((max(group - 1, 1), share, snaps), F32),
            pltpu.VMEM((teams, share, snaps), F32),
            pltpu.VMEM((nz, share, snaps), F32),
            dma(2), dma(2), dma(2), dma(2),
            dma(group - 1), dma(group - 1),
            dma(nz - 1), dma(nz - 1),
            dma(group - 1), dma(group - 1),
            dma(teams - 1), dma(teams - 1), dma(10),
        ],
        compiler_params=pltpu.CompilerParams(
            collective_id=0, has_side_effects=True, vmem_limit_bytes=58 * 1024 * 1024
        ),
        name="vorticity_gram",
    )(velocity.reshape(2, rows, cz), anchor_index.reshape(1, kept))
    modes, basis = pl.pallas_call(
        functools.partial(modes_kernel, dims),
        out_shape=(
            jax.ShapeDtypeStruct((kept * planes * cx, cz), BF16),
            jax.ShapeDtypeStruct((kept, snaps), F32),
        ),
        in_specs=[vmem, hbm, vmem, vmem],
        out_specs=(vmem, vmem),
        scratch_shapes=[
            pltpu.VMEM((snaps, planes * cx * cz), BF16),
            pltpu.VMEM((kept * (planes * cx + 1), cz), F32),
            pltpu.SemaphoreType.DMA,
        ],
        compiler_params=pltpu.CompilerParams(vmem_limit_bytes=58 * 1024 * 1024),
        name="subspace_modes",
    )(gram, flat, snapshot_rank.reshape(1, snaps), start_basis.T)
    return modes.reshape(kept, planes, cx, cz), basis.T


def solution(mesh):
    return jax.shard_map(
        functools.partial(body, mesh.shape["gx"], mesh.shape["gz"]),
        mesh=mesh,
        in_specs=(P(None, None, None, "gx", "gz"), P(), P(), P()),
        out_specs=(P(None, None, "gx", "gz"), P()),
        check_vma=False,
    )
```

```python
import functools
import jax
import jax.numpy as jnp
from jax import lax
from jax.experimental import pallas as pl
from jax.experimental.pallas import tpu as pltpu
from jax.sharding import PartitionSpec as P

ITERS = 3
REACH = 3
MESH = pl.DeviceIdType.MESH
NT = (((1,), (1,)), ((), ()))
F32 = jnp.float32
BF16 = jnp.bfloat16


def iota(shape, dim):
    return lax.broadcasted_iota(jnp.int32, shape, dim)


def stencil_weight(offset):
    size = jnp.abs(offset)
    value = jnp.where(size == 1, 45, jnp.where(size == 2, -9, jnp.where(size == 3, 1, 0)))
    return jnp.where(offset < 0, -value, value).astype(F32).astype(BF16)


def gram_kernel(
    dims, vel_ref, anchor_ref, kept_ref, out_ref,
    flat_ref, spans, streams, spots, wide, uterm, sendx, recvx, sendz, recvz, part, got1, got2, got3,
    sx_sem, rx_sem, sz_sem, rz_sem, s1_sem, r1_sem, s2_sem, r2_sem, s3_sem, r3_sem, s4_sem, r4_sem, load_sem,
):
    snaps, planes, cx, cz, kept, nx, nz, group = dims
    rows = snaps * planes * cx
    stride = planes * cx
    pitch = stride + 1
    me_x = lax.axis_index("gx")
    me_z = lax.axis_index("gz")
    member = lax.rem(me_x, group)
    base = me_x - member
    teams = nx // group
    team = me_x // group
    share = part.shape[0] // group
    xnext, xprev = lax.rem(me_x + 1, nx), lax.rem(me_x + nx - 1, nx)
    znext, zprev = lax.rem(me_z + 1, nz), lax.rem(me_z + nz - 1, nz)

    in_group = [(base + lax.rem(member + d, group), me_z) for d in range(1, group)]
    in_teams = [(lax.rem(team + d, teams) * group + member, me_z) for d in range(1, teams)]
    in_z = [(me_x, lax.rem(me_z + d, nz)) for d in range(1, nz)]
    greet = in_group + in_teams + in_z
    if teams > 1:
        greet = greet + [(xnext, me_z), (xprev, me_z)]

    quarter = rows // 4
    loads = []
    for half, kept_in in ((0, spans), (1, streams)):
        for c in range(4):
            here = pl.ds(c * quarter, quarter)
            loads.append(pltpu.make_async_copy(
                vel_ref.at[half, here], kept_in.at[here], load_sem.at[half * 4 + c]
            ))
    loads.append(pltpu.make_async_copy(anchor_ref, spots, load_sem.at[8]))
    barrier = pltpu.get_barrier_semaphore()
    for peer in greet:
        pl.semaphore_signal(barrier, inc=1, device_id=peer, device_id_type=MESH)
    for copy in loads[:4] + loads[8:]:
        copy.start()

    def remote(src, dst, send, recv, peer):
        return pltpu.make_async_remote_copy(
            src_ref=src, dst_ref=dst, send_sem=send, recv_sem=recv,
            device_id=peer, device_id_type=MESH,
        )

    edge = iota((32, cz), 0)
    lane = iota((32, cz), 1)
    packed = jnp.zeros((32, quarter), F32)
    for c in range(4):
        r = edge % 16 - 4 * c
        wanted = jnp.where(edge < 16, cz - REACH + r, r)
        pick = jnp.where((r >= 0) & (r < REACH) & (lane == wanted), 1.0, 0.0).astype(BF16)
        loads[c].wait()
        loads[4 + c].start()
        packed = packed + lax.dot_general(
            pick, spans[c * quarter : (c + 1) * quarter, :], NT, preferred_element_type=F32
        )
    sendz[...] = packed.astype(BF16).reshape(2, 16, quarter)
    pl.semaphore_wait(barrier, len(greet))
    halos = [
        remote(sendz.at[0], recvz.at[0], sz_sem.at[0], rz_sem.at[0], (me_x, znext)),
        remote(sendz.at[1], recvz.at[1], sz_sem.at[1], rz_sem.at[1], (me_x, zprev)),
        remote(sendx.at[0], recvx.at[0], sx_sem.at[0], rx_sem.at[0], (xnext, me_z)),
        remote(sendx.at[1], recvx.at[1], sx_sem.at[1], rx_sem.at[1], (xprev, me_z)),
    ]
    halos[0].start()
    halos[1].start()

    some = snaps // 4
    for c in range(4):
        loads[4 + c].wait()

        def widen(m, carry, first=c * some):
            at = pl.multiple_of((first + m) * stride, 16)
            wide[pl.ds((first + m) * pitch, stride), :] = streams[pl.ds(at, stride), :].astype(F32)
            return carry

        lax.fori_loop(0, some, widen, 0, unroll=8)
        for p in range(planes):
            for r in range(REACH):
                low = c * some * pitch + p * cx + r
                block = wide[pl.ds(low + cx - REACH, some, stride=pitch), :]
                sendx[0, p * REACH + r, c * some : (c + 1) * some, :] = block.astype(BF16)
                block = wide[pl.ds(low, some, stride=pitch), :]
                sendx[1, p * REACH + r, c * some : (c + 1) * some, :] = block.astype(BF16)
    halos[2].start()
    halos[3].start()

    loads[8].wait()
    index = spots[...]
    total_x, total_z = cx * nx, cz * nz
    plane_of = index // (total_x * total_z)
    remain = index % (total_x * total_z)
    local_x = remain // total_z - me_x * cx
    local_z = remain % total_z - me_z * cz
    owned = (local_x >= 0) & (local_x < cx) & (local_z >= 0) & (local_z < cz)
    position = jnp.where(owned, (plane_of * cx + local_x) * cz + local_z, -1).astype(F32)
    column = jnp.transpose(jnp.broadcast_to(position, (kept, kept)))[:, 0:1]

    band = stencil_weight(iota((cz, cz), 1) - iota((cz, cz), 0))
    halos[0].wait_recv()
    halos[1].wait_recv()
    sides = jnp.transpose(recvz[...].reshape(32, quarter).astype(F32)).astype(BF16)

    def spanwise(c, carry):
        r = edge % 16 - 4 * c
        source = jnp.where(edge < 16, r - REACH, cz + r)
        valid = (r >= 0) & (r < REACH)
        spread = stencil_weight(jnp.where(valid, lane - source, 0))
        here = pl.ds(pl.multiple_of(c * quarter, 16), quarter)
        value = jnp.dot(
            spans[here, :], band, preferred_element_type=F32
        ) + jnp.dot(sides, spread, preferred_element_type=F32)
        for m in range(some):
            at = pl.ds((c * some + m) * pitch, stride)
            uterm[at, :] = value[m * stride : (m + 1) * stride, :]
        return carry

    lax.fori_loop(0, 4, spanwise, 0)

    def snapshots(*spans_x):
        def some_rows(step, carry):
            first = pl.multiple_of(step * 16, 16)
            for p in range(planes):
                layers = {}
                needed = {x + d for begin, end in spans_x for x in range(begin, end) for d in range(-REACH, REACH + 1)}
                for x in sorted(needed):
                    if x < 0:
                        block = recvx[0, p * REACH + x + REACH, pl.ds(first, 16), :].astype(F32)
                    elif x >= cx:
                        block = recvx[1, p * REACH + x - cx, pl.ds(first, 16), :].astype(F32)
                    else:
                        block = wide[pl.ds(first * pitch + p * cx + x, 16, stride=pitch), :]
                    layers[x] = block
                for x in [x for begin, end in spans_x for x in range(begin, end)]:
                    value = 45.0 * (layers[x + 1] - layers[x - 1])
                    value = value - 9.0 * (layers[x + 2] - layers[x - 2])
                    value = value + (layers[x + 3] - layers[x - 3])
                    value = value + uterm[pl.ds(first * pitch + p * cx + x, 16, stride=pitch), :]
                    cell = (p * cx + x) * cz
                    flat_ref[pl.ds(first, 16), cell : cell + cz] = (value * (1.0 / 60.0)).astype(BF16)
            return carry

        lax.fori_loop(0, snaps // 16, some_rows, 0)

    def products(begin, end):
        total = jnp.zeros((snaps + kept, snaps), F32)
        for p in range(planes):
            cell, width = (p * cx + begin) * cz, (end - begin) * cz
            block = flat_ref[:, cell : cell + width]
            cell_in = iota((kept, width), 1).astype(F32) + float(cell)
            mark = jnp.where(cell_in == column, 1.0, 0.0).astype(BF16)
            both = jnp.concatenate([block, mark], axis=0)
            total = total + lax.dot_general(both, block, NT, preferred_element_type=F32)
        return total

    snapshots((REACH, cx - REACH))
    part[...] = products(REACH, cx - REACH)
    halos[2].wait_recv()
    halos[3].wait_recv()
    snapshots((0, REACH), (cx - REACH, cx))
    store = pltpu.make_async_copy(flat_ref, kept_ref, load_sem.at[9])
    store.start()
    part[...] += products(0, REACH) + products(cx - REACH, cx)

    started = list(halos)
    first_stage = []
    for d in range(1, group):
        target = lax.rem(member + d, group)
        first_stage.append(remote(
            part.at[pl.ds(target * share, share)], got1.at[d - 1],
            s1_sem.at[d - 1], r1_sem.at[d - 1], in_group[d - 1],
        ))
    for copy in first_stage:
        copy.start()
    mine = part[pl.ds(member * share, share), :]
    for d, copy in enumerate(first_stage):
        copy.wait_recv()
        mine = mine + got1[d]

    def exchange(value, buffer, place, peers, send, recv):
        buffer[place] = value
        copies = [
            remote(buffer.at[place], buffer.at[place], send.at[d], recv.at[d], peer)
            for d, peer in enumerate(peers)
        ]
        for copy in copies:
            copy.start()
        for copy in copies:
            copy.wait_recv()
        started.extend(copies)
        value = buffer[0]
        for other in range(1, len(peers) + 1):
            value = value + buffer[other]
        return value

    if teams > 1:
        mine = exchange(mine, got2, team, in_teams, s4_sem, r4_sem)
    mine = exchange(mine, got3, me_z, in_z, s2_sem, r2_sem)

    home = pl.ds(member * share, share)
    out_ref[home, :] = mine
    last_stage = [
        remote(out_ref.at[home], out_ref.at[home], s3_sem.at[d], r3_sem.at[d], peer)
        for d, peer in enumerate(in_group)
    ]
    for copy in last_stage:
        copy.start()
    for copy in last_stage:
        copy.wait_recv()
    for copy in started + first_stage + last_stage:
        copy.wait_send()
    store.wait()


def orthonormal_rows(block, pivots):
    kept, snaps = block.shape
    inner = lax.dot_general(
        block, block, NT, precision=lax.Precision.HIGHEST, preferred_element_type=F32
    )
    groups = kept // 8
    left = [inner[8 * h : 8 * h + 8, :] for h in range(groups)]
    right = [block[8 * h : 8 * h + 8, :] for h in range(groups)]
    row_in = iota((8, snaps), 0)
    for k0 in range(0, kept, pivots):
        g, s0 = k0 // 8, k0 % 8
        ahead = range(pivots)
        cols = [
            [None] * g
            + [jnp.broadcast_to(left[h][:, k0 + n : k0 + n + 1], (8, snaps)) for h in range(g, groups)]
            for n in ahead
        ]
        own = [
            [jnp.broadcast_to(cols[n][g][s0 + j : s0 + j + 1, :], (8, snaps)) for n in ahead]
            for j in ahead
        ]
        lrow = [jnp.broadcast_to(left[g][s0 + j : s0 + j + 1, :], (8, kept)) for j in ahead]
        rrow = [jnp.broadcast_to(right[g][s0 + j : s0 + j + 1, :], (8, snaps)) for j in ahead]
        for j in ahead:
            pivot = own[j][j]
            inverse = 1.0 / pivot
            for n in range(j + 1, pivots):
                for m in range(n, pivots):
                    own[n][m] = own[n][m] - (own[j][n] * own[j][m]) * inverse
            for n in range(j + 1, pivots):
                times = own[j][n] * inverse
                lrow[n] = lrow[n] - times[:, :kept] * lrow[j]
                rrow[n] = rrow[n] - times * rrow[j]
                for h in range(g + 1, groups):
                    cols[n][h] = cols[n][h] - times * cols[j][h]
            for h in range(g + 1, groups):
                factor = cols[j][h] * inverse
                left[h] = left[h] - factor[:, :kept] * lrow[j]
                right[h] = right[h] - factor * rrow[j]
            right[g] = jnp.where(row_in == s0 + j, rrow[j] * (inverse * jnp.sqrt(pivot)), right[g])
    return jnp.concatenate(right, axis=0)


def modes_kernel(dims, gram_ref, kept_ref, rank_ref, start_ref, modes_ref, basis_ref, flat_ref, spread, sem):
    snaps, planes, cx, cz, kept, nx, nz, group = dims
    fetch = pltpu.make_async_copy(kept_ref, flat_ref, sem)
    fetch.start()
    cells = float(planes * cx * nx * cz * nz)
    stride = planes * cx
    scale = jnp.where(rank_ref[...] < kept, 1.0, 0.25).astype(F32)
    down = jnp.transpose(jnp.broadcast_to(scale, (snaps, snaps)))
    weighted = down * (gram_ref[0:snaps, :] / cells) * scale

    def iterate(step, rows):
        moved = lax.dot_general(
            rows, weighted, NT, precision=lax.Precision.HIGHEST, preferred_element_type=F32
        )
        return orthonormal_rows(moved, 8)

    rows = lax.fori_loop(0, ITERS, iterate, start_ref[...])
    coef = (scale * rows).astype(BF16)
    anchor = jnp.sum(gram_ref[snaps : snaps + kept, :] * coef.astype(F32), axis=1, keepdims=True)
    orient = anchor / jnp.maximum(jnp.abs(anchor), 1.0)
    basis_ref[...] = rows * orient
    fetch.wait()
    for first in range(0, stride, 4):
        raw = orient * jnp.dot(
            coef, flat_ref[:, first * cz : (first + 4) * cz], preferred_element_type=F32
        )
        for n in range(4):
            spread[pl.ds(first + n, kept, stride=stride + 1), :] = raw[:, n * cz : (n + 1) * cz]

    def narrow(k, carry):
        block = spread[pl.ds(k * (stride + 1), stride), :]
        modes_ref[pl.ds(pl.multiple_of(k * stride, 16), stride), :] = block.astype(BF16)
        return carry

    lax.fori_loop(0, kept, narrow, 0, unroll=8)


def body(nx, nz, velocity, snapshot_rank, anchor_index, start_basis):
    _, snaps, planes, cx, cz = velocity.shape
    kept = start_basis.shape[1]
    total = snaps + kept
    group = max(g for g in (1, 2, 4, 8, 3, 6, 12, 24) if nx % g == 0 and total % (8 * g) == 0)
    dims = (snaps, planes, cx, cz, kept, nx, nz, group)
    rows = snaps * planes * cx
    share = total // group
    teams = nx // group
    vmem = pl.BlockSpec(memory_space=pltpu.VMEM)
    hbm = pl.BlockSpec(memory_space=pltpu.HBM)
    dma = lambda n: pltpu.SemaphoreType.DMA((max(n, 1),))
    flat, gram = pl.pallas_call(
        functools.partial(gram_kernel, dims),
        out_shape=(
            jax.ShapeDtypeStruct((snaps, planes * cx * cz), BF16),
            jax.ShapeDtypeStruct((total, snaps), F32),
        ),
        in_specs=[hbm] * 2,
        out_specs=(hbm, vmem),
        scratch_shapes=[
            pltpu.VMEM((snaps, planes * cx * cz), BF16),
            pltpu.VMEM((rows, cz), BF16),
            pltpu.VMEM((rows, cz), BF16),
            pltpu.VMEM((1, kept), jnp.int32),
            pltpu.VMEM((rows + snaps, cz), F32),
            pltpu.VMEM((rows + snaps, cz), F32),
            pltpu.VMEM((2, planes * REACH, snaps, cz), BF16),
            pltpu.VMEM((2, planes * REACH, snaps, cz), BF16),
            pltpu.VMEM((2, 16, rows // 4), BF16),
            pltpu.VMEM((2, 16, rows // 4), BF16),
            pltpu.VMEM((total, snaps), F32),
            pltpu.VMEM((max(group - 1, 1), share, snaps), F32),
            pltpu.VMEM((teams, share, snaps), F32),
            pltpu.VMEM((nz, share, snaps), F32),
            dma(2), dma(2), dma(2), dma(2),
            dma(group - 1), dma(group - 1),
            dma(nz - 1), dma(nz - 1),
            dma(group - 1), dma(group - 1),
            dma(teams - 1), dma(teams - 1), dma(10),
        ],
        compiler_params=pltpu.CompilerParams(
            collective_id=0, has_side_effects=True, vmem_limit_bytes=58 * 1024 * 1024
        ),
        name="vorticity_gram",
    )(velocity.reshape(2, rows, cz), anchor_index.reshape(1, kept))
    modes, basis = pl.pallas_call(
        functools.partial(modes_kernel, dims),
        out_shape=(
            jax.ShapeDtypeStruct((kept * planes * cx, cz), BF16),
            jax.ShapeDtypeStruct((kept, snaps), F32),
        ),
        in_specs=[vmem, hbm, vmem, vmem],
        out_specs=(vmem, vmem),
        scratch_shapes=[
            pltpu.VMEM((snaps, planes * cx * cz), BF16),
            pltpu.VMEM((kept * (planes * cx + 1), cz), F32),
            pltpu.SemaphoreType.DMA,
        ],
        compiler_params=pltpu.CompilerParams(vmem_limit_bytes=58 * 1024 * 1024),
        name="subspace_modes",
    )(gram, flat, snapshot_rank.reshape(1, snaps), start_basis.T)
    return modes.reshape(kept, planes, cx, cz), basis.T


def solution(mesh):
    return jax.shard_map(
        functools.partial(body, mesh.shape["gx"], mesh.shape["gz"]),
        mesh=mesh,
        in_specs=(P(None, None, None, "gx", "gz"), P(), P(), P()),
        out_specs=(P(None, None, "gx", "gz"), P()),
        check_vma=False,
    )
```
